256 devices in a mesh: dp: 64 (over x, z, y_lo), tensor: 4 (over y_hi, core).
Axes of the slice: x: 4, y: 4 (y_hi: 2, y_lo: 2; y = y_hi * 2 + y_lo), z: 8, core: 2. Of those that a mesh axis runs over, the one named last changes fastest.
Arguments:
- tokens: bfloat16 [32768, 8192], P(('dp', 'tensor')), may hold values from -6 to 6
- gate_pre: bfloat16 [32768, 1024], P('dp', 'tensor'), may hold values from -6 to 6
- up_pre: bfloat16 [32768, 1024], P('dp', 'tensor'), may hold values from -6 to 6
- d_hidden: bfloat16 [32768, 1024], P('dp', 'tensor'), may hold values from -0.032958984 to 0.032958984
- left_roots: bfloat16 [1024, 8, 2, 1024], P('dp'), as said below
- right_roots: bfloat16 [2, 1024, 1024], P(None, 'tensor'), as said below
Outputs:
- update: float32 [1024, 8, 2, 1024], P('dp', None, None, 'tensor')
The draws below stay inside these ranges and needn't reach their ends.
Inputs may be any that keep to these rules, and one draw needn't show every extreme that they name: Every block is symmetric: left_roots[r, b, m, k] equals left_roots[k, b, m, r], and right_roots[m, j, c] equals right_roots[m, c, j]; each block is positive definite. Each right_roots[m] is symmetric and positive definite.
All inputs are finite; a program needn't handle non-finite values.
Results may differ from the reference program's by a relative error of at most 0.005.
Values may be sent and summed in bfloat16 or wider, within the bound.
A program may use at most 128 MiB of HBM per device.

```python
import jax
import jax.numpy as jnp
from jax import lax

D = 8192
BLOCK = 1024
NBLK = 8
FFW = 1024
TOKENS = 32768


def draw_left_roots(key, part):
    key = jax.random.fold_in(key, 11)
    key_off, key_diag = jax.random.split(key, 2)
    noise = jax.random.normal(key_off, (BLOCK, NBLK, 2, BLOCK), jnp.float32)
    offdiag = (noise + noise.transpose(3, 1, 2, 0)) * (0.35 / BLOCK ** 0.5)
    diag_vals = jax.random.uniform(key_diag, (BLOCK, NBLK, 2), jnp.float32, 1.5, 3.0)
    row_ids = jnp.arange(BLOCK)[:, None, None, None]
    col_ids = jnp.arange(BLOCK)[None, None, None, :]
    identity = (row_ids == col_ids).astype(jnp.float32)
    result = offdiag + identity * diag_vals[..., None]
    return result.astype(jnp.bfloat16)


def draw_right_roots(key, part):
    key = jax.random.fold_in(key, 23)
    key_off, key_diag = jax.random.split(key, 2)
    noise = jax.random.normal(key_off, (2, FFW, FFW), jnp.float32)
    offdiag = (noise + noise.transpose(0, 2, 1)) * (0.35 / FFW ** 0.5)
    diag_vals = jax.random.uniform(key_diag, (2, FFW), jnp.float32, 1.5, 3.0)
    row_ids = jnp.arange(FFW)[None, :, None]
    col_ids = jnp.arange(FFW)[None, None, :]
    identity = (row_ids == col_ids).astype(jnp.float32)
    result = offdiag + identity * diag_vals[:, :, None]
    return result.astype(jnp.bfloat16)


def block_scale(key, dims, cuts, low, largest):
    def one(position, shards_of):
        steps = jax.random.uniform(jax.random.fold_in(jax.random.fold_in(key, 6), position), (shards_of,), jnp.float32, low / len(cuts), largest / len(cuts))
        return jnp.repeat(jnp.exp(steps), dims[position] // shards_of).reshape((-1,) + (1,) * (len(dims) - position - 1))

    loudness = one(*cuts[0])
    for cut in cuts[1:]:
        loudness = loudness * one(*cut)
    return loudness


def bell_draw(own_key, extent, spread, bound, shards=(), held_as=jnp.bfloat16):
    drawn = jax.random.normal(own_key, extent, jnp.float32) * spread
    if len(shards) > 0:
        drawn = block_scale(own_key, extent, shards, -0.22, 0.18) * drawn
    return jnp.clip(drawn, min=-bound, max=bound).astype(held_as)


def setup_inputs(seed: int = 0) -> dict:
    seeds = jax.random.split(jax.random.key(seed), 7)
    tokens = bell_draw(seeds[0], (TOKENS, D), 1.0, 6.0, ((0, 256),))
    gate_pre = bell_draw(seeds[1], (TOKENS, FFW), 1.5, 6.0, ((0, 64), (1, 4)))
    up_pre = bell_draw(seeds[2], (TOKENS, FFW), 1.0, 6.0, ((0, 64), (1, 4)))
    d_hidden = bell_draw(seeds[3], (TOKENS, FFW), (1.0 / (TOKENS ** 0.5)), 0.032958984, ((0, 64), (1, 4)))
    left_roots = draw_left_roots(jax.random.fold_in(seeds[6], 71), 0)
    right_roots = draw_right_roots(jax.random.fold_in(seeds[6], 71), 0)
    return dict(tokens=tokens, gate_pre=gate_pre, up_pre=up_pre, d_hidden=d_hidden, left_roots=left_roots, right_roots=right_roots)


def reference(tokens, gate_pre, up_pre, d_hidden, left_roots, right_roots):
    gate_val = gate_pre.astype(jnp.float32)
    up_val = up_pre.astype(jnp.float32)
    cotangent = d_hidden.astype(jnp.float32)
    sig_gate = jax.nn.sigmoid(gate_val)
    d_gate = (cotangent * up_val * sig_gate * (1.0 + gate_val * (1.0 - sig_gate))).astype(jnp.bfloat16)
    d_up = (cotangent * gate_val * sig_gate).astype(jnp.bfloat16)
    stacked = jnp.concatenate([d_gate, d_up], axis=1)
    grad = lax.dot_general(tokens, stacked, (((0,), (0,)), ((), ())), preferred_element_type=jnp.float32)
    grad = grad.reshape(NBLK, BLOCK, 2, FFW).transpose(1, 0, 2, 3)
    grad_low = grad.astype(jnp.bfloat16)
    mixed = jnp.einsum("rbmj,mjc->rbmc", grad_low.astype(jnp.float32), right_roots.astype(jnp.float32))
    mixed = mixed.astype(jnp.bfloat16)
    return jnp.einsum("rbmk,kbmc->rbmc", left_roots.astype(jnp.float32), mixed.astype(jnp.float32))
```

```python
import jax
import jax.numpy as jnp
from jax import lax
from jax.experimental import pallas as pl
from jax.experimental.pallas import tpu as pltpu
from jax.sharding import PartitionSpec as P

MESH = pl.DeviceIdType.MESH
F32 = jnp.float32
BF16 = jnp.bfloat16

NX, NY, NZ = 4, 4, 8
SIZES = (96, 160, 160, 96)
STARTS = tuple(sum(SIZES[:i]) for i in range(len(SIZES)))
CHUNKS = len(SIZES)
HALF = 512


def device(x, y, z, core):
    return ((x * NZ + z) * 2 + lax.rem(y, 2), lax.div(y, 2) * 2 + core)


def ring(value, step, size):
    return lax.rem(value + (step + size), size)


def lane_of(y, core):
    return pl.multiple_of(
        lax.rem(y, 2) * 512 + (lax.div(y, 2) * 2 + core) * 128, 128
    )


def kernel(
    tok_hbm, gate_hbm, up_hbm, dh_hbm, left_hbm, right_hbm, out_ref,
    tok_ref, gate_ref, up_ref, dh_ref, left_ref, dga, tt, tk, fw, part, a_s, a_r, b_s, b_r, z_s, z_r, g_full,
    l1, lb, lg_f, lg_s, xm, rm, out_s,
    dg_send, dg_recv, dx_send, dx_recv, tk_send, tk_recv, tf_send,
    fw_recv, a_send, a_recv, bb_send, bb_recv, zz_send, zz_recv,
    g_send, g_recv, l1_send, l1_recv, l3_send, l3_recv, r_send, r_recv,
    t1_send, t1_recv, t2_send, t2_recv, in_sem,
):
    dp = lax.axis_index("dp")
    tensor = lax.axis_index("tensor")
    y_lo = lax.rem(dp, 2)
    z = lax.rem(lax.div(dp, 2), NZ)
    x = lax.div(dp, 2 * NZ)
    y_hi = lax.div(tensor, 2)
    core = lax.rem(tensor, 2)
    y = y_hi * 2 + y_lo
    other = 1 - core
    xp, xm1, xo = ring(x, 1, NX), ring(x, -1, NX), ring(x, 2, NX)
    yp, ym, yo = ring(y, 1, NY), ring(y, -1, NY), ring(y, 2, NY)

    def send(src, dst, ssem, rsem, dev):
        pltpu.make_async_remote_copy(
            src_ref=src, dst_ref=dst, send_sem=ssem, recv_sem=rsem,
            device_id=dev, device_id_type=MESH,
        ).start()

    def send_or_copy(is_me, src, dst, ssem, rsem, dev):
        @pl.when(is_me)
        def _():
            pltpu.make_async_copy(src, dst, rsem).start()

        @pl.when(jnp.logical_not(is_me))
        def _():
            send(src, dst, ssem, rsem, dev)

    def arrived(dst, rsem):
        pltpu.make_async_remote_copy(
            src_ref=dst, dst_ref=dst, send_sem=rsem, recv_sem=rsem,
            device_id=device(x, y, z, other), device_id_type=MESH,
        ).wait_recv()

    def sent(src, ssem):
        pltpu.make_async_remote_copy(
            src_ref=src, dst_ref=src, send_sem=ssem, recv_sem=ssem,
            device_id=device(x, y, z, other), device_id_type=MESH,
        ).wait_send()

    y_t = y_hi * 2 + core
    mine = lax.rem(x, 2)
    loads = [
        pltpu.make_async_copy(src, dst, in_sem.at[i])
        for i, (src, dst) in enumerate((
            (gate_hbm, gate_ref), (up_hbm, up_ref), (dh_hbm, dh_ref),
            (left_hbm.at[:, pl.ds(2 * y_t, 2)], left_ref), (tok_hbm, tok_ref),
            (right_hbm.at[mine], rm.at[tensor]),
        ))
    ]
    for load in loads:
        load.start()

    barrier = pltpu.get_barrier_semaphore()
    partners = []
    for step_x in range(NX):
        for step_y in range(NY):
            for cc in range(2):
                if step_x or step_y or cc:
                    partners.append(device(
                        ring(x, step_x, NX), ring(y, step_y, NY), z, lax.rem(core + cc, 2)
                    ))
    for step in range(1, NZ):
        partners.append(device(x, y, ring(z, step, NZ), core))
    for partner in partners:
        pl.semaphore_signal(barrier, inc=1, device_id=partner, device_id_type=MESH)

    def elementwise(i, _):
        rows = pl.ds(pl.multiple_of(i * 64, 64), 64)
        g = gate_ref[rows, :].astype(F32)
        u = up_ref[rows, :].astype(F32)
        h = dh_ref[rows, :].astype(F32)
        s = 1.0 / (1.0 + jnp.exp(-g))
        dga[tensor, 0, y_lo, rows, :] = (h * u * s * (1.0 + g * (1.0 - s))).astype(BF16)
        dga[tensor, 1, y_lo, rows, :] = (h * g * s).astype(BF16)
        return 0

    for load in loads[:3]:
        load.wait()
    lax.fori_loop(0, 8, elementwise, 0)
    pl.semaphore_wait(barrier, len(partners))

    def dg(y_from, m):
        return dga.at[lax.div(y_from, 2) * 2 + core, m, lax.rem(y_from, 2)]

    def along(y_from, m, index, y_to):
        send(dg(y_from, m), dg(y_from, m), dg_send, dg_recv.at[index], device(x, y_to, z, core))

    def cross(y_from, m):
        send(dg(y_from, m), dg(y_from, m), dx_send, dx_recv, device(x, y, z, other))

    along(y, 0, 0, yp)
    along(y, 1, 1, ym)
    along(y, 1, 2, yp)
    along(y, 0, 3, ym)
    cross(y, 0)
    cross(y, 1)

    loads[3].wait()
    l_core = lax.div(x, 2)
    l_slot = lax.rem(x, 2) * 2 + y_lo
    for x_t in range(NX):
        is_me = jnp.logical_and(jnp.logical_and(x == x_t, y == y_t), core == l_core)
        l1[x_t] = left_ref[:, x_t // 2, x_t % 2]
        send_or_copy(is_me, l1.at[x_t], lb.at[z, l_slot], l1_send, l1_recv,
                     device(x_t, y_t, z, l_core))

    loads[4].wait()

    def transpose(y_to, _):
        for bl in range(2):
            for cc in range(2):
                for part_of in range(4):
                    column = pl.multiple_of(
                        y_to * 2048 + (bl * 1024 + cc * 512 + part_of * 128), 128
                    )
                    tt[y_to, bl, cc, part_of * 128:(part_of + 1) * 128] = (
                        tok_ref[:, pl.ds(column, 128)].T
                    )
        return 0

    lax.fori_loop(0, NY, transpose, 0)

    def rows_of(kc):
        return pl.ds(STARTS[kc], SIZES[kc])

    def send_tokens(kc):
        rows = rows_of(kc)
        here = tk.at[:, rows, pl.ds(lane_of(y, core), 128)]
        send(tt.at[yo, 0, :, rows], fw.at[0, :, rows], tk_send, fw_recv.at[kc, 0],
             device(x, yp, z, core))
        send(tt.at[yo, 1, :, rows], fw.at[1, :, rows], tk_send, fw_recv.at[kc, 1],
             device(x, ym, z, core))
        for cc in range(2):
            send(tt.at[yp, :, cc, rows], here, tk_send, tk_recv.at[kc], device(x, yp, z, cc))
            send(tt.at[ym, :, cc, rows], here, tk_send, tk_recv.at[kc], device(x, ym, z, cc))
        send(tt.at[y, :, other, rows], here, tk_send, tk_recv.at[kc], device(x, y, z, other))
        pltpu.make_async_copy(tt.at[y, :, core, rows], here, tk_recv.at[kc]).start()

    def forward(kc):
        rows = rows_of(kc)
        for way, y_from, y_to in ((0, ym, yp), (1, yp, ym)):
            arrived(fw.at[way, :, rows], fw_recv.at[kc, way])
            there = tk.at[way, rows, pl.ds(lane_of(y_from, core), 128)]
            for cc in range(2):
                send(fw.at[way, cc, rows], there, tf_send, tk_recv.at[kc],
                     device(x, y_to, z, cc))

    arrived(dg(ym, 0), dg_recv.at[0])
    along(ym, 0, 4, yp)
    arrived(dg(yp, 1), dg_recv.at[1])
    along(yp, 1, 5, ym)
    cross(ym, 0)
    cross(yp, 1)

    zp, zm = ring(z, 1, NZ), ring(z, -1, NZ)

    def left_up(step):
        slot = ring(z, -step, NZ)
        if step > 0:
            arrived(lb.at[slot], l3_recv.at[step - 1])
        if step < 4:
            send(lb.at[slot], lb.at[slot], l3_send, l3_recv.at[step],
                 device(x, y, zp, core))

    def left_down(step):
        slot = ring(z, step, NZ)
        if step > 0:
            arrived(lb.at[slot], l3_recv.at[3 + step])
        if step < 3:
            send(lb.at[slot], lb.at[slot], l3_send, l3_recv.at[4 + step],
                 device(x, y, zm, core))

    arrived(lb.at[z], l1_recv)

    def left_step(step):
        left_up(step)
        if step < 4:
            left_down(step)

    send_tokens(0)
    left_step(0)
    arrived(dg(ym, 1), dg_recv.at[2])
    cross(ym, 1)
    arrived(dg(yp, 0), dg_recv.at[3])
    cross(yp, 0)
    left_step(1)

    arrived(dg(yo, 0), dg_recv.at[4])
    cross(yo, 0)
    arrived(dg(yo, 1), dg_recv.at[5])
    cross(yo, 1)
    forward(0)
    send_tokens(1)
    left_step(2)
    arrived(dga.at[0:2], dx_recv)

    def multiply(kc):
        rows, size = rows_of(kc), SIZES[kc]
        arrived(tk.at[:, rows], tk_recv.at[kc])

        def matrix(m, _):
            for t in range(4):
                total = jnp.dot(
                    tk[:, rows].reshape(2 * size, 1024), dga[t, m].reshape(1024, 256),
                    preferred_element_type=F32,
                )
                for bl in range(2):
                    part[bl * 2 + m, rows, t * 256:(t + 1) * 256] = (
                        total[bl * size:(bl + 1) * size]
                    )
            return 0

        lax.fori_loop(0, 2, matrix, 0)

    def halves(kc):
        start, half = STARTS[kc], SIZES[kc] // 2
        return pl.ds(start, half), pl.ds(start + half, half), pl.ds(start // 2, half)

    def reduce_far(kc):
        rows = rows_of(kc)
        first, second, packed = halves(kc)
        a_s[rows] = part[xo, rows].astype(BF16)
        send(a_s.at[first], a_r.at[0, packed], a_send, a_recv.at[kc, 0],
             device(xp, y, z, core))
        send(a_s.at[second], a_r.at[1, packed], a_send, a_recv.at[kc, 1],
             device(xm1, y, z, core))

    def reduce_near(kc):
        rows = rows_of(kc)
        first, second, packed = halves(kc)
        arrived(a_r.at[0, packed], a_recv.at[kc, 0])
        b_s[0, first] = (part[xp, first] + a_r[0, packed].astype(F32)).astype(BF16)
        b_s[0, second] = part[xp, second].astype(BF16)
        send(b_s.at[0, rows], b_r.at[0, rows], bb_send, bb_recv.at[kc],
             device(xp, y, z, core))
        arrived(a_r.at[1, packed], a_recv.at[kc, 1])
        b_s[1, first] = part[xm1, first].astype(BF16)
        b_s[1, second] = (part[xm1, second] + a_r[1, packed].astype(F32)).astype(BF16)
        send(b_s.at[1, rows], b_r.at[1, rows], bb_send, bb_recv.at[kc],
             device(xm1, y, z, core))

    def reduce_own(kc):
        rows = rows_of(kc)
        arrived(b_r.at[:, rows], bb_recv.at[kc])
        for zt in range(NZ):
            cols = slice(zt * 128, (zt + 1) * 128)
            z_s[zt, rows] = (
                part[x, rows, cols]
                + b_r[0, rows, cols].astype(F32)
                + b_r[1, rows, cols].astype(F32)
            ).astype(BF16)
        for step in range(1, NZ):
            zt = ring(z, step, NZ)
            send(z_s.at[zt, rows], z_r.at[step - 1, rows], zz_send,
                 zz_recv.at[kc], device(x, y, zt, core))

    def reduce_z(kc):
        rows = rows_of(kc)
        arrived(z_r.at[:, rows], zz_recv.at[kc])
        total = z_s[z, rows].astype(F32)
        for i in range(NZ - 1):
            total = total + z_r[i, rows].astype(F32)
        g_full[core, rows] = total.astype(BF16)
        send(g_full.at[core, rows], g_full.at[core, rows], g_send, g_recv.at[kc],
             device(x, y, z, other))

    far = (1 - y_hi) * 2

    def right_send(_):
        loads[5].wait()
        send(rm.at[tensor], rm.at[tensor], r_send, r_recv.at[0],
             device(x, NY - 1 - y, z, core))
        send(rm.at[tensor], rm.at[tensor], r_send, r_recv.at[1],
             device(x, y, z, other))

    def right_cross(_):
        arrived(rm.at[far + core], r_recv.at[0])
        send(rm.at[far + core], rm.at[far + core], r_send, r_recv.at[2],
             device(x, y, z, other))

    def left_times(low, high):
        return sum(
            jnp.dot(
                lb[:, :, :, cc * HALF + low:cc * HALF + high].reshape(512, high - low),
                g_full[cc, low:high], preferred_element_type=F32,
            )
            for cc in range(2)
        )

    def left_most(_):
        for kc in range(3):
            arrived(g_full.at[other, rows_of(kc)], g_recv.at[kc])
        lg_f[...] = left_times(0, 384)

    M, A, B, C, Z = multiply, reduce_far, reduce_near, reduce_own, reduce_z
    F, T = forward, send_tokens
    order = (
        (M, 0), (A, 0), (left_step, 3), (F, 1), (T, 2), (B, 0),
        (M, 1), (A, 1), (left_step, 4), (F, 2), (T, 3), (B, 1), (C, 0),
        (M, 2), (A, 2), (F, 3), (right_send, 0), (B, 2), (C, 1), (Z, 0),
        (M, 3), (A, 3), (C, 2), (Z, 1), (B, 3), (right_cross, 0),
        (C, 3), (Z, 2), (left_most, 0), (Z, 3),
    )
    for step, kc in order:
        step(kc)

    for kc in range(3, CHUNKS):
        arrived(g_full.at[other, rows_of(kc)], g_recv.at[kc])
    product = lg_f[...] + left_times(384, HALF)
    lg_s[...] = product.astype(BF16).reshape(NZ, 64, 128)

    place = pl.ds(pl.multiple_of(z * 128, 128), 128)
    for step in range(1, NZ):
        zt = ring(z, step, NZ)
        send(lg_s.at[zt], xm.at[:, place], t1_send, t1_recv,
             device(x, y, zt, core))
    xm[:, place] = lg_s[z]
    arrived(rm.at[y_hi * 2 + other], r_recv.at[1])
    arrived(rm.at[far + other], r_recv.at[2])
    arrived(lg_s.at[0:NZ - 1], t1_recv)

    block = 2 * y + lax.div(x, 2)
    for yh in range(2):
        for cc in range(2):
            t = yh * 2 + cc
            result = jnp.dot(
                xm[...], rm[:, :, t * 256:(t + 1) * 256].reshape(1024, 256),
                preferred_element_type=F32,
            )
            out_s[t * 4:t * 4 + 4] = result.reshape(4, 16, 256)
            for xl in range(2):
                for yl in range(2):
                    is_me = jnp.logical_and(
                        jnp.logical_and(x == 2 * core + xl, y == 2 * yh + yl), core == cc
                    )
                    piece = xl * 2 + yl
                    send_or_copy(is_me, out_s.at[t * 4 + piece], out_ref.at[mine, block],
                                 t2_send, t2_recv, device(2 * core + xl, 2 * yh + yl, z, cc))

    sent(tt.at[0:3], tk_send)
    sent(tt.at[3, 0], tk_send)
    sent(fw, tf_send)
    sent(dga.at[0], dg_send)
    sent(dga.at[0, 0], dg_send)
    sent(dga.at[0:2], dx_send)
    sent(a_s, a_send)
    sent(b_s, bb_send)
    sent(z_s.at[0:NZ - 1], zz_send)
    sent(g_full.at[0], g_send)
    sent(lb.at[0:NZ - 1], l3_send)
    sent(rm.at[0:3], r_send)
    sent(lg_s.at[0:NZ - 1], t1_send)
    sent(l1.at[0:3], l1_send)
    pl.when(jnp.logical_not(jnp.logical_and(y == y_t, core == l_core)))(
        lambda: sent(l1.at[3], l1_send)
    )
    arrived(out_ref, t2_recv)
    sent(out_s.at[0:15], t2_send)
    pl.when(core != l_core)(lambda: sent(out_s.at[15], t2_send))


def local(tokens, gate_pre, up_pre, d_hidden, left_roots, right_roots):
    dma = pltpu.SemaphoreType.DMA
    vm = pltpu.VMEM
    scratch = [
        vm((128, 8192), BF16), vm((512, 256), BF16), vm((512, 256), BF16),
        vm((512, 256), BF16), vm((16, 2, 2, 1024), BF16),
        vm((4, 2, 2, 512, 256), BF16),
        vm((NY, 2, 2, HALF, 128), BF16),
        vm((2, HALF, 1024), BF16),
        vm((2, 2, HALF, 128), BF16),
        vm((4, HALF, 1024), F32),
        vm((HALF, 1024), BF16),
        vm((2, HALF // 2, 1024), BF16),
        vm((2, HALF, 1024), BF16),
        vm((2, HALF, 1024), BF16),
        vm((NZ, HALF, 128), BF16),
        vm((NZ - 1, HALF, 128), BF16),
        vm((2, HALF, 128), BF16),
        vm((4, 16, 1024), BF16),
        vm((NZ, 4, 16, 1024), BF16),
        vm((512, 128), F32),
        vm((NZ, 64, 128), BF16),
        vm((64, 1024), BF16),
        vm((4, 256, 1024), BF16),
        vm((16, 16, 256), F32),
        dma, dma((6,)), dma, dma,
        dma, dma((CHUNKS,)), dma,
        dma((CHUNKS, 2)),
        dma, dma((CHUNKS, 2)), dma, dma((CHUNKS,)),
        dma, dma((CHUNKS,)), dma, dma((CHUNKS,)),
        dma, dma, dma, dma((NZ - 1,)), dma, dma((3,)),
        dma, dma, dma, dma, dma((6,)),
    ]
    out = pl.pallas_call(
        kernel,
        out_shape=jax.ShapeDtypeStruct((2, 8, 16, 256), F32),
        in_specs=[pl.BlockSpec(memory_space=pltpu.HBM)] * 6,
        out_specs=pl.BlockSpec(memory_space=pltpu.VMEM),
        scratch_shapes=scratch,
        compiler_params=pltpu.CompilerParams(
            collective_id=0, has_side_effects=True, vmem_limit_bytes=60 * 1024 * 1024
        ),
        cost_estimate=pl.CostEstimate(
            flops=4_500_000_000, bytes_accessed=8_000_000, transcendentals=131072
        ),
    )(tokens, gate_pre, up_pre, d_hidden, left_roots, right_roots)
    return out.transpose(2, 1, 0, 3)


def solution(mesh):
    in_specs = (
        P(("dp", "tensor"), None),
        P("dp", "tensor"),
        P("dp", "tensor"),
        P("dp", "tensor"),
        P("dp", None, None, None),
        P(None, "tensor", None),
    )
    out_specs = P("dp", None, None, "tensor")
    return jax.shard_map(local, mesh=mesh, in_specs=in_specs, out_specs=out_specs, check_vma=False)
```

```python
import jax
import jax.numpy as jnp
from jax import lax
from jax.experimental import pallas as pl
from jax.experimental.pallas import tpu as pltpu
from jax.sharding import PartitionSpec as P

MESH = pl.DeviceIdType.MESH
F32 = jnp.float32
BF16 = jnp.bfloat16

NX, NY, NZ = 4, 4, 8
SIZES = (96, 128, 128, 96, 64)
STARTS = tuple(sum(SIZES[:i]) for i in range(len(SIZES)))
CHUNKS = len(SIZES)
HALF = 512


def device(x, y, z, core):
    return ((x * NZ + z) * 2 + lax.rem(y, 2), lax.div(y, 2) * 2 + core)


def ring(value, step, size):
    return lax.rem(value + (step + size), size)


def lane_of(y, core):
    return pl.multiple_of(
        lax.rem(y, 2) * 512 + (lax.div(y, 2) * 2 + core) * 128, 128
    )


def kernel(
    tok_hbm, gate_hbm, up_hbm, dh_hbm, left_hbm, right_hbm, out_ref,
    tok_ref, gate_ref, up_ref, dh_ref, left_ref, dga, tt, tk, fw, part, a_s, a_r, b_s, b_r, z_s, z_r, g_full,
    l1, lb, lg_f, lg_s, xm, rm, out_s,
    dg_send, dg_recv, dx_send, dx_recv, tk_send, tk_recv, tf_send,
    fw_recv, a_send, a_recv, bb_send, bb_recv, zz_send, zz_recv,
    g_send, g_recv, l1_send, l1_recv, l3_send, l3_recv, r_send, r_recv,
    t1_send, t1_recv, t2_send, t2_recv, in_sem,
):
    dp = lax.axis_index("dp")
    tensor = lax.axis_index("tensor")
    y_lo = lax.rem(dp, 2)
    z = lax.rem(lax.div(dp, 2), NZ)
    x = lax.div(dp, 2 * NZ)
    y_hi = lax.div(tensor, 2)
    core = lax.rem(tensor, 2)
    y = y_hi * 2 + y_lo
    other = 1 - core
    xp, xm1, xo = ring(x, 1, NX), ring(x, -1, NX), ring(x, 2, NX)
    yp, ym, yo = ring(y, 1, NY), ring(y, -1, NY), ring(y, 2, NY)

    def send(src, dst, ssem, rsem, dev):
        pltpu.make_async_remote_copy(
            src_ref=src, dst_ref=dst, send_sem=ssem, recv_sem=rsem,
            device_id=dev, device_id_type=MESH,
        ).start()

    def send_or_copy(is_me, src, dst, ssem, rsem, dev):
        @pl.when(is_me)
        def _():
            pltpu.make_async_copy(src, dst, rsem).start()

        @pl.when(jnp.logical_not(is_me))
        def _():
            send(src, dst, ssem, rsem, dev)

    def arrived(dst, rsem):
        pltpu.make_async_remote_copy(
            src_ref=dst, dst_ref=dst, send_sem=rsem, recv_sem=rsem,
            device_id=device(x, y, z, other), device_id_type=MESH,
        ).wait_recv()

    def sent(src, ssem):
        pltpu.make_async_remote_copy(
            src_ref=src, dst_ref=src, send_sem=ssem, recv_sem=ssem,
            device_id=device(x, y, z, other), device_id_type=MESH,
        ).wait_send()

    y_t = y_hi * 2 + core
    mine = lax.rem(x, 2)
    loads = [
        pltpu.make_async_copy(src, dst, in_sem.at[i])
        for i, (src, dst) in enumerate((
            (gate_hbm, gate_ref), (up_hbm, up_ref), (dh_hbm, dh_ref),
            (left_hbm.at[:, pl.ds(2 * y_t, 2)], left_ref), (tok_hbm, tok_ref),
            (right_hbm.at[mine], rm.at[tensor]),
        ))
    ]
    for load in loads:
        load.start()

    barrier = pltpu.get_barrier_semaphore()
    partners = []
    for step_x in range(NX):
        for step_y in range(NY):
            for cc in range(2):
                if step_x or step_y or cc:
                    partners.append(device(
                        ring(x, step_x, NX), ring(y, step_y, NY), z, lax.rem(core + cc, 2)
                    ))
    for step in range(1, NZ):
        partners.append(device(x, y, ring(z, step, NZ), core))
    for partner in partners:
        pl.semaphore_signal(barrier, inc=1, device_id=partner, device_id_type=MESH)

    def elementwise(i, _):
        rows = pl.ds(pl.multiple_of(i * 64, 64), 64)
        g = gate_ref[rows, :].astype(F32)
        u = up_ref[rows, :].astype(F32)
        h = dh_ref[rows, :].astype(F32)
        s = 1.0 / (1.0 + jnp.exp(-g))
        dga[tensor, 0, y_lo, rows, :] = (h * u * s * (1.0 + g * (1.0 - s))).astype(BF16)
        dga[tensor, 1, y_lo, rows, :] = (h * g * s).astype(BF16)
        return 0

    for load in loads[:3]:
        load.wait()
    lax.fori_loop(0, 8, elementwise, 0)
    pl.semaphore_wait(barrier, len(partners))

    def dg(y_from, m):
        return dga.at[lax.div(y_from, 2) * 2 + core, m, lax.rem(y_from, 2)]

    def along(y_from, m, index, y_to):
        send(dg(y_from, m), dg(y_from, m), dg_send, dg_recv.at[index], device(x, y_to, z, core))

    def cross(y_from, m):
        send(dg(y_from, m), dg(y_from, m), dx_send, dx_recv, device(x, y, z, other))

    along(y, 0, 0, yp)
    along(y, 1, 1, ym)
    along(y, 1, 2, yp)
    along(y, 0, 3, ym)
    cross(y, 0)
    cross(y, 1)

    loads[3].wait()
    l_core = lax.div(x, 2)
    l_slot = lax.rem(x, 2) * 2 + y_lo
    for x_t in range(NX):
        is_me = jnp.logical_and(jnp.logical_and(x == x_t, y == y_t), core == l_core)
        l1[x_t] = left_ref[:, x_t // 2, x_t % 2]
        send_or_copy(is_me, l1.at[x_t], lb.at[z, l_slot], l1_send, l1_recv,
                     device(x_t, y_t, z, l_core))

    loads[4].wait()

    def transpose(y_to, _):
        for bl in range(2):
            for cc in range(2):
                for part_of in range(4):
                    column = pl.multiple_of(
                        y_to * 2048 + (bl * 1024 + cc * 512 + part_of * 128), 128
                    )
                    tt[y_to, bl, cc, part_of * 128:(part_of + 1) * 128] = (
                        tok_ref[:, pl.ds(column, 128)].T
                    )
        return 0

    lax.fori_loop(0, NY, transpose, 0)

    def rows_of(kc):
        return pl.ds(STARTS[kc], SIZES[kc])

    def send_tokens(kc):
        rows = rows_of(kc)
        here = tk.at[:, rows, pl.ds(lane_of(y, core), 128)]
        send(tt.at[yo, 0, :, rows], fw.at[0, :, rows], tk_send, fw_recv.at[kc, 0],
             device(x, yp, z, core))
        send(tt.at[yo, 1, :, rows], fw.at[1, :, rows], tk_send, fw_recv.at[kc, 1],
             device(x, ym, z, core))
        for cc in range(2):
            send(tt.at[yp, :, cc, rows], here, tk_send, tk_recv.at[kc], device(x, yp, z, cc))
            send(tt.at[ym, :, cc, rows], here, tk_send, tk_recv.at[kc], device(x, ym, z, cc))
        send(tt.at[y, :, other, rows], here, tk_send, tk_recv.at[kc], device(x, y, z, other))
        pltpu.make_async_copy(tt.at[y, :, core, rows], here, tk_recv.at[kc]).start()

    def forward(kc):
        rows = rows_of(kc)
        for way, y_from, y_to in ((0, ym, yp), (1, yp, ym)):
            arrived(fw.at[way, :, rows], fw_recv.at[kc, way])
            there = tk.at[way, rows, pl.ds(lane_of(y_from, core), 128)]
            for cc in range(2):
                send(fw.at[way, cc, rows], there, tf_send, tk_recv.at[kc],
                     device(x, y_to, z, cc))

    arrived(dg(ym, 0), dg_recv.at[0])
    along(ym, 0, 4, yp)
    arrived(dg(yp, 1), dg_recv.at[1])
    along(yp, 1, 5, ym)
    cross(ym, 0)
    cross(yp, 1)

    zp, zm = ring(z, 1, NZ), ring(z, -1, NZ)

    def left_up(step):
        slot = ring(z, -step, NZ)
        if step > 0:
            arrived(lb.at[slot], l3_recv.at[step - 1])
        if step < 4:
            send(lb.at[slot], lb.at[slot], l3_send, l3_recv.at[step],
                 device(x, y, zp, core))

    def left_down(step):
        slot = ring(z, step, NZ)
        if step > 0:
            arrived(lb.at[slot], l3_recv.at[3 + step])
        if step < 3:
            send(lb.at[slot], lb.at[slot], l3_send, l3_recv.at[4 + step],
                 device(x, y, zm, core))

    def left_step(step):
        left_up(step)
        if step < 4:
            left_down(step)

    send_tokens(0)
    arrived(lb.at[z], l1_recv)
    left_step(0)
    arrived(dg(ym, 1), dg_recv.at[2])
    cross(ym, 1)
    arrived(dg(yp, 0), dg_recv.at[3])
    cross(yp, 0)
    left_step(1)

    arrived(dg(yo, 0), dg_recv.at[4])
    cross(yo, 0)
    arrived(dg(yo, 1), dg_recv.at[5])
    cross(yo, 1)
    forward(0)
    send_tokens(1)
    left_step(2)

    def multiply(kc):
        rows, size = rows_of(kc), SIZES[kc]
        arrived(tk.at[:, rows], tk_recv.at[kc])

        def matrix(turn, _):
            m = lax.rem(mine + turn, 2)
            for t in range(4):
                total = jnp.dot(
                    tk[:, rows].reshape(2 * size, 1024), dga[t, m].reshape(1024, 256),
                    preferred_element_type=F32,
                )
                for bl in range(2):
                    part[bl * 2 + m, rows, t * 256:(t + 1) * 256] = (
                        total[bl * size:(bl + 1) * size]
                    )
            pl.when(turn == 0)(lambda: reduce_far(kc))
            return 0

        lax.fori_loop(0, 2, matrix, 0)

    def halves(kc):
        start, half = STARTS[kc], SIZES[kc] // 2
        return pl.ds(start, half), pl.ds(start + half, half), pl.ds(start // 2, half)

    def reduce_far(kc):
        rows = rows_of(kc)
        first, second, packed = halves(kc)
        a_s[rows] = part[xo, rows].astype(BF16)
        send(a_s.at[first], a_r.at[0, packed], a_send, a_recv.at[kc, 0],
             device(xp, y, z, core))
        send(a_s.at[second], a_r.at[1, packed], a_send, a_recv.at[kc, 1],
             device(xm1, y, z, core))

    def near_plain(kc):
        first, second, _ = halves(kc)
        for way, x_to, plain in ((0, xp, second), (1, xm1, first)):
            b_s[way, plain] = part[x_to, plain].astype(BF16)
            send(b_s.at[way, plain], b_r.at[way, plain], bb_send, bb_recv.at[kc],
                 device(x_to, y, z, core))

    def near_sum(kc):
        first, second, packed = halves(kc)
        for way, x_to, summed in ((0, xp, first), (1, xm1, second)):
            arrived(a_r.at[way, packed], a_recv.at[kc, way])
            b_s[way, summed] = (
                part[x_to, summed] + a_r[way, packed].astype(F32)
            ).astype(BF16)
            send(b_s.at[way, summed], b_r.at[way, summed], bb_send, bb_recv.at[kc],
                 device(x_to, y, z, core))

    def reduce_own(kc):
        rows = rows_of(kc)
        arrived(b_r.at[:, rows], bb_recv.at[kc])
        for zt in range(NZ):
            cols = slice(zt * 128, (zt + 1) * 128)
            z_s[zt, rows] = (
                part[x, rows, cols]
                + b_r[0, rows, cols].astype(F32)
                + b_r[1, rows, cols].astype(F32)
            ).astype(BF16)
        for step in range(1, NZ):
            zt = ring(z, step, NZ)
            send(z_s.at[zt, rows], z_r.at[step - 1, rows], zz_send,
                 zz_recv.at[kc], device(x, y, zt, core))

    def reduce_z(kc):
        rows = rows_of(kc)
        arrived(z_r.at[:, rows], zz_recv.at[kc])
        total = z_s[z, rows].astype(F32)
        for i in range(NZ - 1):
            total = total + z_r[i, rows].astype(F32)
        g_full[core, rows] = total.astype(BF16)
        send(g_full.at[core, rows], g_full.at[core, rows], g_send, g_recv.at[kc],
             device(x, y, z, other))

    far = (1 - y_hi) * 2

    def right_send(_):
        loads[5].wait()
        send(rm.at[tensor], rm.at[tensor], r_send, r_recv.at[0],
             device(x, NY - 1 - y, z, core))
        send(rm.at[tensor], rm.at[tensor], r_send, r_recv.at[1],
             device(x, y, z, other))

    def right_cross(_):
        arrived(rm.at[far + core], r_recv.at[0])
        send(rm.at[far + core], rm.at[far + core], r_send, r_recv.at[2],
             device(x, y, z, other))

    def left_times(low, high):
        return sum(
            jnp.dot(
                lb[:, :, :, cc * HALF + low:cc * HALF + high].reshape(512, high - low),
                g_full[cc, low:high], preferred_element_type=F32,
            )
            for cc in range(2)
        )

    def left_most(_):
        for kc in range(4):
            arrived(g_full.at[other, rows_of(kc)], g_recv.at[kc])
        lg_f[...] = left_times(0, 384)

    def gathered(_):
        arrived(dga.at[0:2], dx_recv)

    M, B, S, C, Z = multiply, near_plain, near_sum, reduce_own, reduce_z
    F, T = forward, send_tokens
    order = (
        (F, 1), (T, 2), (gathered, 0), (M, 0), (B, 0), (left_step, 3), (S, 0),
        (F, 2), (T, 3), (M, 1), (B, 1), (left_step, 4), (S, 1), (C, 0),
        (F, 3), (T, 4), (M, 2), (B, 2), (S, 2), (C, 1), (Z, 0),
        (F, 4), (right_send, 0), (M, 3), (B, 3), (S, 3), (C, 2), (Z, 1),
        (M, 4), (B, 4), (S, 4), (C, 3), (Z, 2), (right_cross, 0),
        (C, 4), (Z, 3), (left_most, 0), (Z, 4),
    )
    for step, kc in order:
        step(kc)

    for kc in range(4, CHUNKS):
        arrived(g_full.at[other, rows_of(kc)], g_recv.at[kc])
    product = lg_f[...] + left_times(384, HALF)
    lg_s[...] = product.astype(BF16).reshape(NZ, 64, 128)

    place = pl.ds(pl.multiple_of(z * 128, 128), 128)
    for step in range(1, NZ):
        zt = ring(z, step, NZ)
        send(lg_s.at[zt], xm.at[:, place], t1_send, t1_recv,
             device(x, y, zt, core))
    xm[:, place] = lg_s[z]
    arrived(rm.at[y_hi * 2 + other], r_recv.at[1])
    arrived(rm.at[far + other], r_recv.at[2])
    arrived(lg_s.at[0:NZ - 1], t1_recv)

    block = 2 * y + lax.div(x, 2)
    for yh in range(2):
        for cc in range(2):
            t = yh * 2 + cc
            result = jnp.dot(
                xm[...], rm[:, :, t * 256:(t + 1) * 256].reshape(1024, 256),
                preferred_element_type=F32,
            )
            out_s[t * 4:t * 4 + 4] = result.reshape(4, 16, 256)
            for xl in range(2):
                for yl in range(2):
                    is_me = jnp.logical_and(
                        jnp.logical_and(x == 2 * core + xl, y == 2 * yh + yl), core == cc
                    )
                    piece = xl * 2 + yl
                    send_or_copy(is_me, out_s.at[t * 4 + piece], out_ref.at[mine, block],
                                 t2_send, t2_recv, device(2 * core + xl, 2 * yh + yl, z, cc))

    sent(tt.at[0:3], tk_send)
    sent(tt.at[3, 0], tk_send)
    sent(fw, tf_send)
    sent(dga.at[0], dg_send)
    sent(dga.at[0, 0], dg_send)
    sent(dga.at[0:2], dx_send)
    sent(a_s, a_send)
    sent(b_s, bb_send)
    sent(z_s.at[0:NZ - 1], zz_send)
    sent(g_full.at[0], g_send)
    sent(lb.at[0:NZ - 1], l3_send)
    sent(rm.at[0:3], r_send)
    sent(lg_s.at[0:NZ - 1], t1_send)
    sent(l1.at[0:3], l1_send)
    pl.when(jnp.logical_not(jnp.logical_and(y == y_t, core == l_core)))(
        lambda: sent(l1.at[3], l1_send)
    )
    arrived(out_ref, t2_recv)
    sent(out_s.at[0:15], t2_send)
    pl.when(core != l_core)(lambda: sent(out_s.at[15], t2_send))


def local(tokens, gate_pre, up_pre, d_hidden, left_roots, right_roots):
    dma = pltpu.SemaphoreType.DMA
    vm = pltpu.VMEM
    scratch = [
        vm((128, 8192), BF16), vm((512, 256), BF16), vm((512, 256), BF16),
        vm((512, 256), BF16), vm((16, 2, 2, 1024), BF16),
        vm((4, 2, 2, 512, 256), BF16),
        vm((NY, 2, 2, HALF, 128), BF16),
        vm((2, HALF, 1024), BF16),
        vm((2, 2, HALF, 128), BF16),
        vm((4, HALF, 1024), F32),
        vm((HALF, 1024), BF16),
        vm((2, HALF // 2, 1024), BF16),
        vm((2, HALF, 1024), BF16),
        vm((2, HALF, 1024), BF16),
        vm((NZ, HALF, 128), BF16),
        vm((NZ - 1, HALF, 128), BF16),
        vm((2, HALF, 128), BF16),
        vm((4, 16, 1024), BF16),
        vm((NZ, 4, 16, 1024), BF16),
        vm((512, 128), F32),
        vm((NZ, 64, 128), BF16),
        vm((64, 1024), BF16),
        vm((4, 256, 1024), BF16),
        vm((16, 16, 256), F32),
        dma, dma((6,)), dma, dma,
        dma, dma((CHUNKS,)), dma,
        dma((CHUNKS, 2)),
        dma, dma((CHUNKS, 2)), dma, dma((CHUNKS,)),
        dma, dma((CHUNKS,)), dma, dma((CHUNKS,)),
        dma, dma, dma, dma((NZ - 1,)), dma, dma((3,)),
        dma, dma, dma, dma, dma((6,)),
    ]
    out = pl.pallas_call(
        kernel,
        out_shape=jax.ShapeDtypeStruct((2, 8, 16, 256), F32),
        in_specs=[pl.BlockSpec(memory_space=pltpu.HBM)] * 6,
        out_specs=pl.BlockSpec(memory_space=pltpu.VMEM),
        scratch_shapes=scratch,
        compiler_params=pltpu.CompilerParams(
            collective_id=0, has_side_effects=True, vmem_limit_bytes=60 * 1024 * 1024
        ),
        cost_estimate=pl.CostEstimate(
            flops=4_500_000_000, bytes_accessed=8_000_000, transcendentals=131072
        ),
    )(tokens, gate_pre, up_pre, d_hidden, left_roots, right_roots)
    return out.transpose(2, 1, 0, 3)


def solution(mesh):
    in_specs = (
        P(("dp", "tensor"), None),
        P("dp", "tensor"),
        P("dp", "tensor"),
        P("dp", "tensor"),
        P("dp", None, None, None),
        P(None, "tensor", None),
    )
    out_specs = P("dp", None, None, "tensor")
    return jax.shard_map(local, mesh=mesh, in_specs=in_specs, out_specs=out_specs, check_vma=False)
```

```python
import jax
import jax.numpy as jnp
from jax import lax
from jax.experimental import pallas as pl
from jax.experimental.pallas import tpu as pltpu
from jax.sharding import PartitionSpec as P

MESH = pl.DeviceIdType.MESH
F32 = jnp.float32
BF16 = jnp.bfloat16

NX, NY, NZ = 4, 4, 8
SIZES = (96, 128, 128, 128, 32)
STARTS = tuple(sum(SIZES[:i]) for i in range(len(SIZES)))
CHUNKS = len(SIZES)
HALF = 512
FAR_FIRST = (4, 3, 5, 2, 6, 1, 7)


def device(x, y, z, core):
    return ((x * NZ + z) * 2 + lax.rem(y, 2), lax.div(y, 2) * 2 + core)


def ring(value, step, size):
    return lax.rem(value + (step + size), size)


def lane_of(y, core):
    return pl.multiple_of(
        lax.rem(y, 2) * 512 + (lax.div(y, 2) * 2 + core) * 128, 128
    )


def kernel(
    tok_hbm, gate_hbm, up_hbm, dh_hbm, left_hbm, right_hbm, out_ref,
    tok_ref, gate_ref, up_ref, dh_ref, left_ref, dga, tt, tk, fw, part, a_s, a_r, b_s, b_r, z_s, z_r, g_full,
    l1, lb, lg_f, lg_s, xm, rm, out_s,
    dg_send, dg_recv, dx_send, dx_recv, tk_send, tk_recv, tf_send,
    fw_recv, a_send, a_recv, bb_send, bb_recv, zz_send, zz_recv,
    g_send, g_recv, l1_send, l1_recv, l3_send, l3_recv, r_send, r_recv,
    t1_send, t1_recv, t2_send, t2_recv, in_sem,
):
    dp = lax.axis_index("dp")
    tensor = lax.axis_index("tensor")
    y_lo = lax.rem(dp, 2)
    z = lax.rem(lax.div(dp, 2), NZ)
    x = lax.div(dp, 2 * NZ)
    y_hi = lax.div(tensor, 2)
    core = lax.rem(tensor, 2)
    y = y_hi * 2 + y_lo
    other = 1 - core
    xp, xm1, xo = ring(x, 1, NX), ring(x, -1, NX), ring(x, 2, NX)
    yp, ym, yo = ring(y, 1, NY), ring(y, -1, NY), ring(y, 2, NY)

    def send(src, dst, ssem, rsem, dev):
        pltpu.make_async_remote_copy(
            src_ref=src, dst_ref=dst, send_sem=ssem, recv_sem=rsem,
            device_id=dev, device_id_type=MESH,
        ).start()

    def send_or_copy(is_me, src, dst, ssem, rsem, dev):
        @pl.when(is_me)
        def _():
            pltpu.make_async_copy(src, dst, rsem).start()

        @pl.when(jnp.logical_not(is_me))
        def _():
            send(src, dst, ssem, rsem, dev)

    def arrived(dst, rsem):
        pltpu.make_async_remote_copy(
            src_ref=dst, dst_ref=dst, send_sem=rsem, recv_sem=rsem,
            device_id=device(x, y, z, other), device_id_type=MESH,
        ).wait_recv()

    def sent(src, ssem):
        pltpu.make_async_remote_copy(
            src_ref=src, dst_ref=src, send_sem=ssem, recv_sem=ssem,
            device_id=device(x, y, z, other), device_id_type=MESH,
        ).wait_send()

    y_t = y_hi * 2 + core
    mine = lax.rem(x, 2)
    loads = [
        pltpu.make_async_copy(src, dst, in_sem.at[i])
        for i, (src, dst) in enumerate((
            (gate_hbm, gate_ref), (up_hbm, up_ref), (dh_hbm, dh_ref),
            (left_hbm.at[:, pl.ds(2 * y_t, 2)], left_ref), (tok_hbm, tok_ref),
            (right_hbm.at[mine], rm.at[tensor]),
        ))
    ]
    for load in loads:
        load.start()

    barrier = pltpu.get_barrier_semaphore()
    partners = []
    for step_x in range(NX):
        for step_y in range(NY):
            for cc in range(2):
                if step_x or step_y or cc:
                    partners.append(device(
                        ring(x, step_x, NX), ring(y, step_y, NY), z, lax.rem(core + cc, 2)
                    ))
    for step in range(1, NZ):
        partners.append(device(x, y, ring(z, step, NZ), core))
    for partner in partners:
        pl.semaphore_signal(barrier, inc=1, device_id=partner, device_id_type=MESH)

    def elementwise(i, _):
        rows = pl.ds(pl.multiple_of(i * 64, 64), 64)
        g = gate_ref[rows, :].astype(F32)
        u = up_ref[rows, :].astype(F32)
        h = dh_ref[rows, :].astype(F32)
        s = 1.0 / (1.0 + jnp.exp(-g))
        dga[tensor, 0, y_lo, rows, :] = (h * u * s * (1.0 + g * (1.0 - s))).astype(BF16)
        dga[tensor, 1, y_lo, rows, :] = (h * g * s).astype(BF16)
        return 0

    for load in loads[:3]:
        load.wait()
    lax.fori_loop(0, 8, elementwise, 0)
    pl.semaphore_wait(barrier, len(partners))

    def dg(y_from, m):
        return dga.at[lax.div(y_from, 2) * 2 + core, m, lax.rem(y_from, 2)]

    def along(y_from, m, index, y_to):
        send(dg(y_from, m), dg(y_from, m), dg_send, dg_recv.at[index], device(x, y_to, z, core))

    def cross(y_from, m):
        send(dg(y_from, m), dg(y_from, m), dx_send, dx_recv, device(x, y, z, other))

    along(y, 0, 0, yp)
    along(y, 1, 1, ym)
    along(y, 1, 2, yp)
    along(y, 0, 3, ym)
    cross(y, 0)
    cross(y, 1)

    loads[3].wait()
    l_core = lax.div(x, 2)
    l_slot = lax.rem(x, 2) * 2 + y_lo
    for x_t in range(NX):
        is_me = jnp.logical_and(jnp.logical_and(x == x_t, y == y_t), core == l_core)
        l1[x_t] = left_ref[:, x_t // 2, x_t % 2]
        send_or_copy(is_me, l1.at[x_t], lb.at[z, l_slot], l1_send, l1_recv,
                     device(x_t, y_t, z, l_core))

    loads[4].wait()

    def transpose(y_to, _):
        for bl in range(2):
            for cc in range(2):
                for part_of in range(4):
                    column = pl.multiple_of(
                        y_to * 2048 + (bl * 1024 + cc * 512 + part_of * 128), 128
                    )
                    tt[y_to, bl, cc, part_of * 128:(part_of + 1) * 128] = (
                        tok_ref[:, pl.ds(column, 128)].T
                    )
        return 0

    lax.fori_loop(0, NY, transpose, 0)

    def rows_of(kc):
        return pl.ds(STARTS[kc], SIZES[kc])

    def send_tokens(kc):
        rows = rows_of(kc)
        here = tk.at[:, rows, pl.ds(lane_of(y, core), 128)]
        send(tt.at[yo, 0, :, rows], fw.at[0, :, rows], tk_send, fw_recv.at[kc, 0],
             device(x, yp, z, core))
        send(tt.at[yo, 1, :, rows], fw.at[1, :, rows], tk_send, fw_recv.at[kc, 1],
             device(x, ym, z, core))
        for cc in range(2):
            send(tt.at[yp, :, cc, rows], here, tk_send, tk_recv.at[kc], device(x, yp, z, cc))
            send(tt.at[ym, :, cc, rows], here, tk_send, tk_recv.at[kc], device(x, ym, z, cc))
        send(tt.at[y, :, other, rows], here, tk_send, tk_recv.at[kc], device(x, y, z, other))
        pltpu.make_async_copy(tt.at[y, :, core, rows], here, tk_recv.at[kc]).start()

    def forward(kc):
        rows = rows_of(kc)
        for way, y_from, y_to in ((0, ym, yp), (1, yp, ym)):
            arrived(fw.at[way, :, rows], fw_recv.at[kc, way])
            there = tk.at[way, rows, pl.ds(lane_of(y_from, core), 128)]
            for cc in range(2):
                send(fw.at[way, cc, rows], there, tf_send, tk_recv.at[kc],
                     device(x, y_to, z, cc))

    arrived(dg(ym, 0), dg_recv.at[0])
    along(ym, 0, 4, yp)
    arrived(dg(yp, 1), dg_recv.at[1])
    along(yp, 1, 5, ym)
    cross(ym, 0)
    cross(yp, 1)

    zp, zm = ring(z, 1, NZ), ring(z, -1, NZ)

    def left_up(step):
        slot = ring(z, -step, NZ)
        if step > 0:
            arrived(lb.at[slot], l3_recv.at[step - 1])
        if step < 4:
            send(lb.at[slot], lb.at[slot], l3_send, l3_recv.at[step],
                 device(x, y, zp, core))

    def left_down(step):
        slot = ring(z, step, NZ)
        if step > 0:
            arrived(lb.at[slot], l3_recv.at[3 + step])
        if step < 3:
            send(lb.at[slot], lb.at[slot], l3_send, l3_recv.at[4 + step],
                 device(x, y, zm, core))

    def left_step(step):
        left_up(step)
        if step < 4:
            left_down(step)

    send_tokens(0)
    arrived(lb.at[z], l1_recv)
    left_step(0)
    arrived(dg(ym, 1), dg_recv.at[2])
    cross(ym, 1)
    arrived(dg(yp, 0), dg_recv.at[3])
    cross(yp, 0)
    left_step(1)

    arrived(dg(yo, 0), dg_recv.at[4])
    cross(yo, 0)
    arrived(dg(yo, 1), dg_recv.at[5])
    cross(yo, 1)
    forward(0)
    send_tokens(1)
    left_step(2)

    def multiply(kc):
        rows, size = rows_of(kc), SIZES[kc]
        arrived(tk.at[:, rows], tk_recv.at[kc])

        def matrix(turn, _):
            m = lax.rem(mine + turn, 2)
            for t in range(4):
                total = jnp.dot(
                    tk[:, rows].reshape(2 * size, 1024), dga[t, m].reshape(1024, 256),
                    preferred_element_type=F32,
                )
                for bl in range(2):
                    part[bl * 2 + m, rows, t * 256:(t + 1) * 256] = (
                        total[bl * size:(bl + 1) * size]
                    )
            pl.when(turn == 0)(lambda: reduce_far(kc))
            return 0

        lax.fori_loop(0, 2, matrix, 0)

    def halves(kc):
        start, half = STARTS[kc], SIZES[kc] // 2
        return pl.ds(start, half), pl.ds(start + half, half), pl.ds(start // 2, half)

    def reduce_far(kc):
        rows = rows_of(kc)
        first, second, packed = halves(kc)
        a_s[rows] = part[xo, rows].astype(BF16)
        send(a_s.at[first], a_r.at[0, packed], a_send, a_recv.at[kc, 0],
             device(xp, y, z, core))
        send(a_s.at[second], a_r.at[1, packed], a_send, a_recv.at[kc, 1],
             device(xm1, y, z, core))

    def near_plain(kc):
        first, second, _ = halves(kc)
        for way, x_to, plain in ((0, xp, second), (1, xm1, first)):
            b_s[way, plain] = part[x_to, plain].astype(BF16)
            send(b_s.at[way, plain], b_r.at[way, plain], bb_send, bb_recv.at[kc],
                 device(x_to, y, z, core))

    def near_sum(kc):
        first, second, packed = halves(kc)
        for way, x_to, summed in ((0, xp, first), (1, xm1, second)):
            arrived(a_r.at[way, packed], a_recv.at[kc, way])
            b_s[way, summed] = (
                part[x_to, summed] + a_r[way, packed].astype(F32)
            ).astype(BF16)
            send(b_s.at[way, summed], b_r.at[way, summed], bb_send, bb_recv.at[kc],
                 device(x_to, y, z, core))

    def reduce_own(kc):
        rows = rows_of(kc)
        arrived(b_r.at[:, rows], bb_recv.at[kc])
        for zt in range(NZ):
            cols = slice(zt * 128, (zt + 1) * 128)
            z_s[zt, rows] = (
                part[x, rows, cols]
                + b_r[0, rows, cols].astype(F32)
                + b_r[1, rows, cols].astype(F32)
            ).astype(BF16)
        for step in FAR_FIRST:
            zt = ring(z, step, NZ)
            send(z_s.at[zt, rows], z_r.at[step - 1, rows], zz_send,
                 zz_recv.at[kc], device(x, y, zt, core))

    def reduce_z(kc):
        rows = rows_of(kc)
        arrived(z_r.at[:, rows], zz_recv.at[kc])
        total = z_s[z, rows].astype(F32)
        for i in range(NZ - 1):
            total = total + z_r[i, rows].astype(F32)
        g_full[core, rows] = total.astype(BF16)
        send(g_full.at[core, rows], g_full.at[core, rows], g_send, g_recv.at[kc],
             device(x, y, z, other))

    far = (1 - y_hi) * 2

    def right_send(_):
        loads[5].wait()
        send(rm.at[tensor], rm.at[tensor], r_send, r_recv.at[0],
             device(x, NY - 1 - y, z, core))
        send(rm.at[tensor], rm.at[tensor], r_send, r_recv.at[1],
             device(x, y, z, other))

    def right_cross(_):
        arrived(rm.at[far + core], r_recv.at[0])
        send(rm.at[far + core], rm.at[far + core], r_send, r_recv.at[2],
             device(x, y, z, other))

    def left_times(way, low, high):
        return sum(
            jnp.dot(
                lb[:, 2 * way:2 * way + 2, :, cc * HALF + low:cc * HALF + high].reshape(
                    256, high - low
                ),
                g_full[cc, low:high], preferred_element_type=F32,
            )
            for cc in range(2)
        )

    def left_most(_):
        for kc in range(4):
            arrived(g_full.at[other, rows_of(kc)], g_recv.at[kc])
        for way in range(2):
            lg_f[way] = left_times(way, 0, 384)

    def gathered(_):
        arrived(dga.at[0:2], dx_recv)

    M, B, S, C, Z = multiply, near_plain, near_sum, reduce_own, reduce_z
    F, T = forward, send_tokens
    order = (
        (F, 1), (T, 2), (gathered, 0), (M, 0), (B, 0), (left_step, 3), (S, 0),
        (F, 2), (T, 3), (M, 1), (B, 1), (left_step, 4), (S, 1), (C, 0),
        (F, 3), (T, 4), (M, 2), (B, 2), (S, 2), (C, 1), (Z, 0),
        (F, 4), (right_send, 0), (M, 3), (B, 3), (S, 3), (C, 2), (Z, 1),
        (M, 4), (B, 4), (S, 4), (C, 3), (Z, 2), (right_cross, 0),
        (C, 4), (Z, 3), (left_most, 0), (Z, 4),
    )
    for step, kc in order:
        step(kc)

    for kc in range(4, CHUNKS):
        arrived(g_full.at[other, rows_of(kc)], g_recv.at[kc])
    place = pl.ds(pl.multiple_of(z * 128, 128), 128)
    for way in range(2):
        some = slice(32 * way, 32 * way + 32)
        product = lg_f[way] + left_times(way, 384, HALF)
        lg_s[:, some] = product.astype(BF16).reshape(NZ, 32, 128)
        for step in FAR_FIRST:
            zt = ring(z, step, NZ)
            send(lg_s.at[zt, some], xm.at[some, place], t1_send, t1_recv.at[way],
                 device(x, y, zt, core))
        xm[some, place] = lg_s[z, some]
    arrived(rm.at[y_hi * 2 + other], r_recv.at[1])
    arrived(rm.at[far + other], r_recv.at[2])

    block = 2 * y + lax.div(x, 2)
    for xl in range(2):
        some = slice(32 * xl, 32 * xl + 32)
        arrived(lg_s.at[0:NZ - 1, some], t1_recv.at[xl])
        for yh in range(2):
            for cc in range(2):
                t = yh * 2 + cc
                result = jnp.dot(
                    xm[some], rm[:, :, t * 256:(t + 1) * 256].reshape(1024, 256),
                    preferred_element_type=F32,
                )
                first = xl * 8 + t * 2
                out_s[first:first + 2] = result.reshape(2, 16, 256)
                for yl in range(2):
                    is_me = jnp.logical_and(
                        jnp.logical_and(x == 2 * core + xl, y == 2 * yh + yl), core == cc
                    )
                    send_or_copy(is_me, out_s.at[first + yl], out_ref.at[mine, block],
                                 t2_send, t2_recv, device(2 * core + xl, 2 * yh + yl, z, cc))

    sent(tt.at[0:3], tk_send)
    sent(tt.at[3, 0], tk_send)
    sent(fw, tf_send)
    sent(dga.at[0], dg_send)
    sent(dga.at[0, 0], dg_send)
    sent(dga.at[0:2], dx_send)
    sent(a_s, a_send)
    sent(b_s, bb_send)
    sent(z_s.at[0:NZ - 1], zz_send)
    sent(g_full.at[0], g_send)
    sent(lb.at[0:NZ - 1], l3_send)
    sent(rm.at[0:3], r_send)
    sent(lg_s.at[0:NZ - 1], t1_send)
    sent(l1.at[0:3], l1_send)
    pl.when(jnp.logical_not(jnp.logical_and(y == y_t, core == l_core)))(
        lambda: sent(l1.at[3], l1_send)
    )
    arrived(out_ref, t2_recv)
    sent(out_s.at[0:15], t2_send)
    pl.when(core != l_core)(lambda: sent(out_s.at[15], t2_send))


def local(tokens, gate_pre, up_pre, d_hidden, left_roots, right_roots):
    dma = pltpu.SemaphoreType.DMA
    vm = pltpu.VMEM
    scratch = [
        vm((128, 8192), BF16), vm((512, 256), BF16), vm((512, 256), BF16),
        vm((512, 256), BF16), vm((16, 2, 2, 1024), BF16),
        vm((4, 2, 2, 512, 256), BF16),
        vm((NY, 2, 2, HALF, 128), BF16),
        vm((2, HALF, 1024), BF16),
        vm((2, 2, HALF, 128), BF16),
        vm((4, HALF, 1024), F32),
        vm((HALF, 1024), BF16),
        vm((2, HALF // 2, 1024), BF16),
        vm((2, HALF, 1024), BF16),
        vm((2, HALF, 1024), BF16),
        vm((NZ, HALF, 128), BF16),
        vm((NZ - 1, HALF, 128), BF16),
        vm((2, HALF, 128), BF16),
        vm((4, 16, 1024), BF16),
        vm((NZ, 4, 16, 1024), BF16),
        vm((2, 256, 128), F32),
        vm((NZ, 64, 128), BF16),
        vm((64, 1024), BF16),
        vm((4, 256, 1024), BF16),
        vm((16, 16, 256), F32),
        dma, dma((6,)), dma, dma,
        dma, dma((CHUNKS,)), dma,
        dma((CHUNKS, 2)),
        dma, dma((CHUNKS, 2)), dma, dma((CHUNKS,)),
        dma, dma((CHUNKS,)), dma, dma((CHUNKS,)),
        dma, dma, dma, dma((NZ - 1,)), dma, dma((3,)),
        dma, dma((2,)), dma, dma, dma((6,)),
    ]
    out = pl.pallas_call(
        kernel,
        out_shape=jax.ShapeDtypeStruct((2, 8, 16, 256), F32),
        in_specs=[pl.BlockSpec(memory_space=pltpu.HBM)] * 6,
        out_specs=pl.BlockSpec(memory_space=pltpu.VMEM),
        scratch_shapes=scratch,
        compiler_params=pltpu.CompilerParams(
            collective_id=0, has_side_effects=True, vmem_limit_bytes=60 * 1024 * 1024
        ),
        cost_estimate=pl.CostEstimate(
            flops=4_500_000_000, bytes_accessed=8_000_000, transcendentals=131072
        ),
    )(tokens, gate_pre, up_pre, d_hidden, left_roots, right_roots)
    return out.transpose(2, 1, 0, 3)


def solution(mesh):
    in_specs = (
        P(("dp", "tensor"), None),
        P("dp", "tensor"),
        P("dp", "tensor"),
        P("dp", "tensor"),
        P("dp", None, None, None),
        P(None, "tensor", None),
    )
    out_specs = P("dp", None, None, "tensor")
    return jax.shard_map(local, mesh=mesh, in_specs=in_specs, out_specs=out_specs, check_vma=False)
```

```python
import jax
import jax.numpy as jnp
from jax import lax
from jax.experimental import pallas as pl
from jax.experimental.pallas import tpu as pltpu
from jax.sharding import PartitionSpec as P

MESH = pl.DeviceIdType.MESH
F32 = jnp.float32
BF16 = jnp.bfloat16

NX, NY, NZ = 4, 4, 8
SIZES = (96, 128, 128, 128, 32)
STARTS = tuple(sum(SIZES[:i]) for i in range(len(SIZES)))
CHUNKS = len(SIZES)
HALF = 512
FAR_FIRST = (4, 3, 5, 2, 6, 1, 7)


def device(x, y, z, core):
    return ((x * NZ + z) * 2 + lax.rem(y, 2), lax.div(y, 2) * 2 + core)


def ring(value, step, size):
    return lax.rem(value + (step + size), size)


def lane_of(y, core):
    return pl.multiple_of(
        lax.rem(y, 2) * 512 + (lax.div(y, 2) * 2 + core) * 128, 128
    )


def kernel(
    tok_hbm, gate_hbm, up_hbm, dh_hbm, left_hbm, right_hbm, out_ref,
    tok_ref, gate_ref, up_ref, dh_ref, left_ref, dga, tt, tk, fw, part, a_s, a_r, b_s, b_r, z_s, z_r, g_full,
    l1, lb, lg_f, lg_s, xm, rm, out_s,
    dg_send, dg_recv, dx_send, dx_recv, tk_send, tk_recv, tf_send,
    fw_recv, a_send, a_recv, bb_send, bb_recv, zz_send, zz_recv,
    g_send, g_recv, l1_send, l1_recv, l3_send, l3_recv, r_send, r_recv,
    t1_send, t1_recv, t2_send, t2_recv, in_sem,
):
    dp = lax.axis_index("dp")
    tensor = lax.axis_index("tensor")
    y_lo = lax.rem(dp, 2)
    z = lax.rem(lax.div(dp, 2), NZ)
    x = lax.div(dp, 2 * NZ)
    y_hi = lax.div(tensor, 2)
    core = lax.rem(tensor, 2)
    y = y_hi * 2 + y_lo
    other = 1 - core
    xp, xm1, xo = ring(x, 1, NX), ring(x, -1, NX), ring(x, 2, NX)
    yp, ym, yo = ring(y, 1, NY), ring(y, -1, NY), ring(y, 2, NY)

    def send(src, dst, ssem, rsem, dev):
        pltpu.make_async_remote_copy(
            src_ref=src, dst_ref=dst, send_sem=ssem, recv_sem=rsem,
            device_id=dev, device_id_type=MESH,
        ).start()

    def send_or_copy(is_me, src, dst, ssem, rsem, dev):
        @pl.when(is_me)
        def _():
            pltpu.make_async_copy(src, dst, rsem).start()

        @pl.when(jnp.logical_not(is_me))
        def _():
            send(src, dst, ssem, rsem, dev)

    def arrived(dst, rsem):
        pltpu.make_async_remote_copy(
            src_ref=dst, dst_ref=dst, send_sem=rsem, recv_sem=rsem,
            device_id=device(x, y, z, other), device_id_type=MESH,
        ).wait_recv()

    def sent(src, ssem):
        pltpu.make_async_remote_copy(
            src_ref=src, dst_ref=src, send_sem=ssem, recv_sem=ssem,
            device_id=device(x, y, z, other), device_id_type=MESH,
        ).wait_send()

    y_t = y_hi * 2 + core
    mine = lax.rem(x, 2)
    loads = [
        pltpu.make_async_copy(src, dst, in_sem.at[i])
        for i, (src, dst) in enumerate((
            (gate_hbm, gate_ref), (up_hbm, up_ref), (dh_hbm, dh_ref),
            (left_hbm.at[:, pl.ds(2 * y_t, 2)], left_ref), (tok_hbm, tok_ref),
            (right_hbm.at[mine], rm.at[tensor]),
        ))
    ]
    for load in loads:
        load.start()

    barrier = pltpu.get_barrier_semaphore()
    partners = []
    for step_x in range(NX):
        for step_y in range(NY):
            for cc in range(2):
                if step_x or step_y or cc:
                    partners.append(device(
                        ring(x, step_x, NX), ring(y, step_y, NY), z, lax.rem(core + cc, 2)
                    ))
    for step in range(1, NZ):
        partners.append(device(x, y, ring(z, step, NZ), core))
    for partner in partners:
        pl.semaphore_signal(barrier, inc=1, device_id=partner, device_id_type=MESH)

    def elementwise(i, _):
        rows = pl.ds(pl.multiple_of(i * 64, 64), 64)
        g = gate_ref[rows, :].astype(F32)
        u = up_ref[rows, :].astype(F32)
        h = dh_ref[rows, :].astype(F32)
        s = 1.0 / (1.0 + jnp.exp(-g))
        dga[tensor, 0, y_lo, rows, :] = (h * u * s * (1.0 + g * (1.0 - s))).astype(BF16)
        dga[tensor, 1, y_lo, rows, :] = (h * g * s).astype(BF16)
        return 0

    for load in loads[:3]:
        load.wait()
    lax.fori_loop(0, 8, elementwise, 0)
    pl.semaphore_wait(barrier, len(partners))

    def dg(y_from, m):
        return dga.at[lax.div(y_from, 2) * 2 + core, m, lax.rem(y_from, 2)]

    def along(y_from, m, index, y_to):
        send(dg(y_from, m), dg(y_from, m), dg_send, dg_recv.at[index], device(x, y_to, z, core))

    def cross(y_from, m):
        send(dg(y_from, m), dg(y_from, m), dx_send, dx_recv, device(x, y, z, other))

    along(y, 0, 0, yp)
    along(y, 1, 1, ym)
    along(y, 1, 2, yp)
    along(y, 0, 3, ym)
    cross(y, 0)
    cross(y, 1)

    loads[3].wait()
    l_core = lax.div(x, 2)
    l_slot = lax.rem(x, 2) * 2 + y_lo
    for x_t in range(NX):
        is_me = jnp.logical_and(jnp.logical_and(x == x_t, y == y_t), core == l_core)
        l1[x_t] = left_ref[:, x_t // 2, x_t % 2]
        send_or_copy(is_me, l1.at[x_t], lb.at[z, l_slot], l1_send, l1_recv,
                     device(x_t, y_t, z, l_core))

    loads[4].wait()

    def transpose(y_to, _):
        for bl in range(2):
            for cc in range(2):
                for part_of in range(4):
                    column = pl.multiple_of(
                        y_to * 2048 + (bl * 1024 + cc * 512 + part_of * 128), 128
                    )
                    tt[y_to, bl, cc, part_of * 128:(part_of + 1) * 128] = (
                        tok_ref[:, pl.ds(column, 128)].T
                    )
        return 0

    lax.fori_loop(0, NY, transpose, 0)

    def rows_of(kc):
        return pl.ds(STARTS[kc], SIZES[kc])

    def send_tokens(kc):
        rows = rows_of(kc)
        here = tk.at[:, rows, pl.ds(lane_of(y, core), 128)]
        send(tt.at[yo, 0, :, rows], fw.at[0, :, rows], tk_send, fw_recv.at[kc, 0],
             device(x, yp, z, core))
        send(tt.at[yo, 1, :, rows], fw.at[1, :, rows], tk_send, fw_recv.at[kc, 1],
             device(x, ym, z, core))
        for cc in range(2):
            send(tt.at[yp, :, cc, rows], here, tk_send, tk_recv.at[kc], device(x, yp, z, cc))
            send(tt.at[ym, :, cc, rows], here, tk_send, tk_recv.at[kc], device(x, ym, z, cc))
        send(tt.at[y, :, other, rows], here, tk_send, tk_recv.at[kc], device(x, y, z, other))
        pltpu.make_async_copy(tt.at[y, :, core, rows], here, tk_recv.at[kc]).start()

    def forward(kc):
        rows = rows_of(kc)
        for way, y_from, y_to in ((0, ym, yp), (1, yp, ym)):
            arrived(fw.at[way, :, rows], fw_recv.at[kc, way])
            there = tk.at[way, rows, pl.ds(lane_of(y_from, core), 128)]
            for cc in range(2):
                send(fw.at[way, cc, rows], there, tf_send, tk_recv.at[kc],
                     device(x, y_to, z, cc))

    arrived(dg(ym, 0), dg_recv.at[0])
    along(ym, 0, 4, yp)
    arrived(dg(yp, 1), dg_recv.at[1])
    along(yp, 1, 5, ym)
    cross(ym, 0)
    cross(yp, 1)

    zp, zm = ring(z, 1, NZ), ring(z, -1, NZ)

    def left_up(step):
        slot = ring(z, -step, NZ)
        if step > 0:
            arrived(lb.at[slot], l3_recv.at[step - 1])
        if step < 4:
            send(lb.at[slot], lb.at[slot], l3_send, l3_recv.at[step],
                 device(x, y, zp, core))

    def left_down(step):
        slot = ring(z, step, NZ)
        if step > 0:
            arrived(lb.at[slot], l3_recv.at[3 + step])
        if step < 3:
            send(lb.at[slot], lb.at[slot], l3_send, l3_recv.at[4 + step],
                 device(x, y, zm, core))

    def left_step(step):
        left_up(step)
        if step < 4:
            left_down(step)

    send_tokens(0)
    arrived(lb.at[z], l1_recv)
    left_step(0)
    arrived(dg(ym, 1), dg_recv.at[2])
    cross(ym, 1)
    arrived(dg(yp, 0), dg_recv.at[3])
    cross(yp, 0)
    left_step(1)

    arrived(dg(yo, 0), dg_recv.at[4])
    cross(yo, 0)
    arrived(dg(yo, 1), dg_recv.at[5])
    cross(yo, 1)
    forward(0)
    send_tokens(1)
    left_step(2)

    def multiply(kc):
        rows, size = rows_of(kc), SIZES[kc]
        arrived(tk.at[:, rows], tk_recv.at[kc])

        def matrix(turn, _):
            m = lax.rem(mine + turn, 2)
            for t in range(4):
                total = jnp.dot(
                    tk[:, rows].reshape(2 * size, 1024), dga[t, m].reshape(1024, 256),
                    preferred_element_type=F32,
                )
                for bl in range(2):
                    part[bl * 2 + m, rows, t * 256:(t + 1) * 256] = (
                        total[bl * size:(bl + 1) * size]
                    )

            @pl.when(turn == 0)
            def _():
                reduce_far(kc)
                if kc < 2:
                    forward(kc + 1)
                    send_tokens(kc + 2)

            return 0

        lax.fori_loop(0, 2, matrix, 0)

    def halves(kc):
        start, half = STARTS[kc], SIZES[kc] // 2
        return pl.ds(start, half), pl.ds(start + half, half), pl.ds(start // 2, half)

    def reduce_far(kc):
        rows = rows_of(kc)
        first, second, packed = halves(kc)
        a_s[rows] = part[xo, rows].astype(BF16)
        send(a_s.at[first], a_r.at[0, packed], a_send, a_recv.at[kc, 0],
             device(xp, y, z, core))
        send(a_s.at[second], a_r.at[1, packed], a_send, a_recv.at[kc, 1],
             device(xm1, y, z, core))

    def near_plain(kc):
        first, second, _ = halves(kc)
        for way, x_to, plain in ((0, xp, second), (1, xm1, first)):
            b_s[way, plain] = part[x_to, plain].astype(BF16)
            send(b_s.at[way, plain], b_r.at[way, plain], bb_send, bb_recv.at[kc],
                 device(x_to, y, z, core))

    def near_sum(kc):
        first, second, packed = halves(kc)
        for way, x_to, summed in ((0, xp, first), (1, xm1, second)):
            arrived(a_r.at[way, packed], a_recv.at[kc, way])
            b_s[way, summed] = (
                part[x_to, summed] + a_r[way, packed].astype(F32)
            ).astype(BF16)
            send(b_s.at[way, summed], b_r.at[way, summed], bb_send, bb_recv.at[kc],
                 device(x_to, y, z, core))

    def reduce_own(kc):
        rows = rows_of(kc)
        arrived(b_r.at[:, rows], bb_recv.at[kc])
        for zt in range(NZ):
            cols = slice(zt * 128, (zt + 1) * 128)
            z_s[zt, rows] = (
                part[x, rows, cols]
                + b_r[0, rows, cols].astype(F32)
                + b_r[1, rows, cols].astype(F32)
            ).astype(BF16)
        for step in FAR_FIRST:
            zt = ring(z, step, NZ)
            send(z_s.at[zt, rows], z_r.at[step - 1, rows], zz_send,
                 zz_recv.at[kc], device(x, y, zt, core))

    def reduce_z(kc):
        rows = rows_of(kc)
        arrived(z_r.at[:, rows], zz_recv.at[kc])
        total = z_s[z, rows].astype(F32)
        for i in range(NZ - 1):
            total = total + z_r[i, rows].astype(F32)
        g_full[core, rows] = total.astype(BF16)
        send(g_full.at[core, rows], g_full.at[core, rows], g_send, g_recv.at[kc],
             device(x, y, z, other))

    far = (1 - y_hi) * 2

    def right_send(_):
        loads[5].wait()
        send(rm.at[tensor], rm.at[tensor], r_send, r_recv.at[0],
             device(x, NY - 1 - y, z, core))
        send(rm.at[tensor], rm.at[tensor], r_send, r_recv.at[1],
             device(x, y, z, other))

    def right_cross(_):
        arrived(rm.at[far + core], r_recv.at[0])
        send(rm.at[far + core], rm.at[far + core], r_send, r_recv.at[2],
             device(x, y, z, other))

    def left_times(way, low, high):
        return sum(
            jnp.dot(
                lb[:, 2 * way:2 * way + 2, :, cc * HALF + low:cc * HALF + high].reshape(
                    256, high - low
                ),
                g_full[cc, low:high], preferred_element_type=F32,
            )
            for cc in range(2)
        )

    def left_most(_):
        for kc in range(4):
            arrived(g_full.at[other, rows_of(kc)], g_recv.at[kc])
        for way in range(2):
            lg_f[way] = left_times(way, 0, 384)

    def gathered(_):
        arrived(dga.at[0:2], dx_recv)

    M, B, S, C, Z = multiply, near_plain, near_sum, reduce_own, reduce_z
    F, T = forward, send_tokens
    order = (
        (gathered, 0), (M, 0), (B, 0), (left_step, 3), (S, 0),
        (M, 1), (B, 1), (left_step, 4), (S, 1), (C, 0),
        (F, 3), (T, 4), (M, 2), (B, 2), (S, 2), (C, 1), (Z, 0),
        (F, 4), (right_send, 0), (M, 3), (B, 3), (S, 3), (C, 2), (Z, 1),
        (M, 4), (B, 4), (S, 4), (C, 3), (Z, 2), (right_cross, 0),
        (C, 4), (Z, 3), (left_most, 0), (Z, 4),
    )
    for step, kc in order:
        step(kc)

    for kc in range(4, CHUNKS):
        arrived(g_full.at[other, rows_of(kc)], g_recv.at[kc])
    place = pl.ds(pl.multiple_of(z * 128, 128), 128)
    for way in range(2):
        some = slice(32 * way, 32 * way + 32)
        product = lg_f[way] + left_times(way, 384, HALF)
        lg_s[:, some] = product.astype(BF16).reshape(NZ, 32, 128)
        for step in FAR_FIRST:
            zt = ring(z, step, NZ)
            send(lg_s.at[zt, some], xm.at[some, place], t1_send, t1_recv.at[way],
                 device(x, y, zt, core))
        xm[some, place] = lg_s[z, some]
    arrived(rm.at[y_hi * 2 + other], r_recv.at[1])
    arrived(rm.at[far + other], r_recv.at[2])

    block = 2 * y + lax.div(x, 2)
    for xl in range(2):
        some = slice(32 * xl, 32 * xl + 32)
        arrived(lg_s.at[0:NZ - 1, some], t1_recv.at[xl])
        for yh in range(2):
            for cc in range(2):
                t = yh * 2 + cc
                result = jnp.dot(
                    xm[some], rm[:, :, t * 256:(t + 1) * 256].reshape(1024, 256),
                    preferred_element_type=F32,
                )
                first = xl * 8 + t * 2
                out_s[first:first + 2] = result.reshape(2, 16, 256)
                for yl in range(2):
                    is_me = jnp.logical_and(
                        jnp.logical_and(x == 2 * core + xl, y == 2 * yh + yl), core == cc
                    )
                    send_or_copy(is_me, out_s.at[first + yl], out_ref.at[mine, block],
                                 t2_send, t2_recv, device(2 * core + xl, 2 * yh + yl, z, cc))

    sent(tt.at[0:3], tk_send)
    sent(tt.at[3, 0], tk_send)
    sent(fw, tf_send)
    sent(dga.at[0], dg_send)
    sent(dga.at[0, 0], dg_send)
    sent(dga.at[0:2], dx_send)
    sent(a_s, a_send)
    sent(b_s, bb_send)
    sent(z_s.at[0:NZ - 1], zz_send)
    sent(g_full.at[0], g_send)
    sent(lb.at[0:NZ - 1], l3_send)
    sent(rm.at[0:3], r_send)
    sent(lg_s.at[0:NZ - 1], t1_send)
    sent(l1.at[0:3], l1_send)
    pl.when(jnp.logical_not(jnp.logical_and(y == y_t, core == l_core)))(
        lambda: sent(l1.at[3], l1_send)
    )
    arrived(out_ref, t2_recv)
    sent(out_s.at[0:15], t2_send)
    pl.when(core != l_core)(lambda: sent(out_s.at[15], t2_send))


def local(tokens, gate_pre, up_pre, d_hidden, left_roots, right_roots):
    dma = pltpu.SemaphoreType.DMA
    vm = pltpu.VMEM
    scratch = [
        vm((128, 8192), BF16), vm((512, 256), BF16), vm((512, 256), BF16),
        vm((512, 256), BF16), vm((16, 2, 2, 1024), BF16),
        vm((4, 2, 2, 512, 256), BF16),
        vm((NY, 2, 2, HALF, 128), BF16),
        vm((2, HALF, 1024), BF16),
        vm((2, 2, HALF, 128), BF16),
        vm((4, HALF, 1024), F32),
        vm((HALF, 1024), BF16),
        vm((2, HALF // 2, 1024), BF16),
        vm((2, HALF, 1024), BF16),
        vm((2, HALF, 1024), BF16),
        vm((NZ, HALF, 128), BF16),
        vm((NZ - 1, HALF, 128), BF16),
        vm((2, HALF, 128), BF16),
        vm((4, 16, 1024), BF16),
        vm((NZ, 4, 16, 1024), BF16),
        vm((2, 256, 128), F32),
        vm((NZ, 64, 128), BF16),
        vm((64, 1024), BF16),
        vm((4, 256, 1024), BF16),
        vm((16, 16, 256), F32),
        dma, dma((6,)), dma, dma,
        dma, dma((CHUNKS,)), dma,
        dma((CHUNKS, 2)),
        dma, dma((CHUNKS, 2)), dma, dma((CHUNKS,)),
        dma, dma((CHUNKS,)), dma, dma((CHUNKS,)),
        dma, dma, dma, dma((NZ - 1,)), dma, dma((3,)),
        dma, dma((2,)), dma, dma, dma((6,)),
    ]
    out = pl.pallas_call(
        kernel,
        out_shape=jax.ShapeDtypeStruct((2, 8, 16, 256), F32),
        in_specs=[pl.BlockSpec(memory_space=pltpu.HBM)] * 6,
        out_specs=pl.BlockSpec(memory_space=pltpu.VMEM),
        scratch_shapes=scratch,
        compiler_params=pltpu.CompilerParams(
            collective_id=0, has_side_effects=True, vmem_limit_bytes=60 * 1024 * 1024
        ),
        cost_estimate=pl.CostEstimate(
            flops=4_500_000_000, bytes_accessed=8_000_000, transcendentals=131072
        ),
    )(tokens, gate_pre, up_pre, d_hidden, left_roots, right_roots)
    return out.transpose(2, 1, 0, 3)


def solution(mesh):
    in_specs = (
        P(("dp", "tensor"), None),
        P("dp", "tensor"),
        P("dp", "tensor"),
        P("dp", "tensor"),
        P("dp", None, None, None),
        P(None, "tensor", None),
    )
    out_specs = P("dp", None, None, "tensor")
    return jax.shard_map(local, mesh=mesh, in_specs=in_specs, out_specs=out_specs, check_vma=False)
```

```python
import jax
import jax.numpy as jnp
from jax import lax
from jax.experimental import pallas as pl
from jax.experimental.pallas import tpu as pltpu
from jax.sharding import PartitionSpec as P

MESH = pl.DeviceIdType.MESH
F32 = jnp.float32
BF16 = jnp.bfloat16

NX, NY, NZ = 4, 4, 8
SIZES = (96, 128, 128, 128, 32)
STARTS = tuple(sum(SIZES[:i]) for i in range(len(SIZES)))
CHUNKS = len(SIZES)
HALF = 512
FAR_FIRST = (4, 3, 5, 2, 6, 1, 7)


def device(x, y, z, core):
    return ((x * NZ + z) * 2 + lax.rem(y, 2), lax.div(y, 2) * 2 + core)


def ring(value, step, size):
    return lax.rem(value + (step + size), size)


def lane_of(y, core):
    return pl.multiple_of(
        lax.rem(y, 2) * 512 + (lax.div(y, 2) * 2 + core) * 128, 128
    )


def kernel(
    tok_hbm, gate_hbm, up_hbm, dh_hbm, left_hbm, right_hbm, out_ref,
    tok_ref, gate_ref, up_ref, dh_ref, left_ref, dga, tt, tk, fw, part, a_s, a_r, b_s, b_r, z_s, z_r, g_full,
    l1, lb, lg_f, lg_s, xm, rm, out_s,
    dg_send, dg_recv, dx_send, dx_recv, tk_send, tk_recv, tf_send,
    fw_recv, a_send, a_recv, bb_send, bb_recv, zz_send, zz_recv,
    g_send, g_recv, l1_send, l1_recv, l3_send, l3_recv, r_send, r_recv,
    t1_send, t1_recv, t2_send, t2_recv, in_sem,
):
    dp = lax.axis_index("dp")
    tensor = lax.axis_index("tensor")
    y_lo = lax.rem(dp, 2)
    z = lax.rem(lax.div(dp, 2), NZ)
    x = lax.div(dp, 2 * NZ)
    y_hi = lax.div(tensor, 2)
    core = lax.rem(tensor, 2)
    y = y_hi * 2 + y_lo
    other = 1 - core
    xp, xm1, xo = ring(x, 1, NX), ring(x, -1, NX), ring(x, 2, NX)
    yp, ym, yo = ring(y, 1, NY), ring(y, -1, NY), ring(y, 2, NY)

    def send(src, dst, ssem, rsem, dev):
        pltpu.make_async_remote_copy(
            src_ref=src, dst_ref=dst, send_sem=ssem, recv_sem=rsem,
            device_id=dev, device_id_type=MESH,
        ).start()

    def send_or_copy(is_me, src, dst, ssem, rsem, dev):
        @pl.when(is_me)
        def _():
            pltpu.make_async_copy(src, dst, rsem).start()

        @pl.when(jnp.logical_not(is_me))
        def _():
            send(src, dst, ssem, rsem, dev)

    def arrived(dst, rsem):
        pltpu.make_async_remote_copy(
            src_ref=dst, dst_ref=dst, send_sem=rsem, recv_sem=rsem,
            device_id=device(x, y, z, other), device_id_type=MESH,
        ).wait_recv()

    def sent(src, ssem):
        pltpu.make_async_remote_copy(
            src_ref=src, dst_ref=src, send_sem=ssem, recv_sem=ssem,
            device_id=device(x, y, z, other), device_id_type=MESH,
        ).wait_send()

    y_t = y_hi * 2 + core
    mine = lax.rem(x, 2)
    loads = [
        pltpu.make_async_copy(src, dst, in_sem.at[i])
        for i, (src, dst) in enumerate((
            (gate_hbm, gate_ref), (up_hbm, up_ref), (dh_hbm, dh_ref),
            (left_hbm.at[:, pl.ds(2 * y_t, 2)], left_ref), (tok_hbm, tok_ref),
            (right_hbm.at[mine], rm.at[tensor]),
        ))
    ]
    for load in loads:
        load.start()

    barrier = pltpu.get_barrier_semaphore()
    partners = []
    for step_x in range(NX):
        for step_y in range(NY):
            for cc in range(2):
                if step_x or step_y or cc:
                    partners.append(device(
                        ring(x, step_x, NX), ring(y, step_y, NY), z, lax.rem(core + cc, 2)
                    ))
    for step in range(1, NZ):
        partners.append(device(x, y, ring(z, step, NZ), core))
    for partner in partners:
        pl.semaphore_signal(barrier, inc=1, device_id=partner, device_id_type=MESH)

    def elementwise(i, _):
        rows = pl.ds(pl.multiple_of(i * 64, 64), 64)
        g = gate_ref[rows, :].astype(F32)
        u = up_ref[rows, :].astype(F32)
        h = dh_ref[rows, :].astype(F32)
        s = 1.0 / (1.0 + jnp.exp(-g))
        dga[tensor, 0, y_lo, rows, :] = (h * u * s * (1.0 + g * (1.0 - s))).astype(BF16)
        dga[tensor, 1, y_lo, rows, :] = (h * g * s).astype(BF16)
        return 0

    for load in loads[:3]:
        load.wait()
    lax.fori_loop(0, 8, elementwise, 0)
    pl.semaphore_wait(barrier, len(partners))

    def dg(y_from, m):
        return dga.at[lax.div(y_from, 2) * 2 + core, m, lax.rem(y_from, 2)]

    def along(y_from, m, index, y_to):
        send(dg(y_from, m), dg(y_from, m), dg_send, dg_recv.at[index], device(x, y_to, z, core))

    def cross(y_from, m):
        send(dg(y_from, m), dg(y_from, m), dx_send, dx_recv, device(x, y, z, other))

    along(y, 0, 0, yp)
    along(y, 1, 1, ym)
    along(y, 1, 2, yp)
    along(y, 0, 3, ym)
    cross(y, 0)
    cross(y, 1)

    loads[3].wait()
    l_core = lax.div(x, 2)
    l_slot = lax.rem(x, 2) * 2 + y_lo
    for x_t in range(NX):
        is_me = jnp.logical_and(jnp.logical_and(x == x_t, y == y_t), core == l_core)
        l1[x_t] = left_ref[:, x_t // 2, x_t % 2]
        send_or_copy(is_me, l1.at[x_t], lb.at[z, l_slot], l1_send, l1_recv,
                     device(x_t, y_t, z, l_core))

    loads[4].wait()

    def transpose(y_to, _):
        for bl in range(2):
            for cc in range(2):
                for part_of in range(4):
                    column = pl.multiple_of(
                        y_to * 2048 + (bl * 1024 + cc * 512 + part_of * 128), 128
                    )
                    tt[y_to, bl, cc, part_of * 128:(part_of + 1) * 128] = (
                        tok_ref[:, pl.ds(column, 128)].T
                    )
        return 0

    lax.fori_loop(0, NY, transpose, 0)

    def rows_of(kc):
        return pl.ds(STARTS[kc], SIZES[kc])

    def send_tokens(kc):
        rows = rows_of(kc)
        here = tk.at[:, rows, pl.ds(lane_of(y, core), 128)]
        send(tt.at[yo, 0, :, rows], fw.at[0, :, rows], tk_send, fw_recv.at[kc, 0],
             device(x, yp, z, core))
        send(tt.at[yo, 1, :, rows], fw.at[1, :, rows], tk_send, fw_recv.at[kc, 1],
             device(x, ym, z, core))
        for cc in range(2):
            send(tt.at[yp, :, cc, rows], here, tk_send, tk_recv.at[kc], device(x, yp, z, cc))
            send(tt.at[ym, :, cc, rows], here, tk_send, tk_recv.at[kc], device(x, ym, z, cc))
        send(tt.at[y, :, other, rows], here, tk_send, tk_recv.at[kc], device(x, y, z, other))
        pltpu.make_async_copy(tt.at[y, :, core, rows], here, tk_recv.at[kc]).start()

    def forward(kc):
        rows = rows_of(kc)
        for way, y_from, y_to in ((0, ym, yp), (1, yp, ym)):
            arrived(fw.at[way, :, rows], fw_recv.at[kc, way])
            there = tk.at[way, rows, pl.ds(lane_of(y_from, core), 128)]
            for cc in range(2):
                send(fw.at[way, cc, rows], there, tf_send, tk_recv.at[kc],
                     device(x, y_to, z, cc))

    arrived(dg(ym, 0), dg_recv.at[0])
    along(ym, 0, 4, yp)
    arrived(dg(yp, 1), dg_recv.at[1])
    along(yp, 1, 5, ym)
    cross(ym, 0)
    cross(yp, 1)

    zp, zm = ring(z, 1, NZ), ring(z, -1, NZ)

    def left_up(step):
        slot = ring(z, -step, NZ)
        if step > 0:
            arrived(lb.at[slot], l3_recv.at[step - 1])
        if step < 4:
            send(lb.at[slot], lb.at[slot], l3_send, l3_recv.at[step],
                 device(x, y, zp, core))

    def left_down(step):
        slot = ring(z, step, NZ)
        if step > 0:
            arrived(lb.at[slot], l3_recv.at[3 + step])
        if step < 3:
            send(lb.at[slot], lb.at[slot], l3_send, l3_recv.at[4 + step],
                 device(x, y, zm, core))

    def left_step(step):
        left_up(step)
        if step < 4:
            left_down(step)

    send_tokens(0)
    arrived(lb.at[z], l1_recv)
    left_step(0)
    arrived(dg(ym, 1), dg_recv.at[2])
    cross(ym, 1)
    arrived(dg(yp, 0), dg_recv.at[3])
    cross(yp, 0)
    left_step(1)

    arrived(dg(yo, 0), dg_recv.at[4])
    cross(yo, 0)
    arrived(dg(yo, 1), dg_recv.at[5])
    cross(yo, 1)
    forward(0)
    send_tokens(1)
    left_step(2)

    def multiply(kc):
        rows, size = rows_of(kc), SIZES[kc]
        arrived(tk.at[:, rows], tk_recv.at[kc])

        def matrix(turn, _):
            m = lax.rem(mine + turn, 2)
            for t in range(4):
                total = jnp.dot(
                    tk[:, rows].reshape(2 * size, 1024), dga[t, m].reshape(1024, 256),
                    preferred_element_type=F32,
                )
                for bl in range(2):
                    part[bl * 2 + m, rows, t * 256:(t + 1) * 256] = (
                        total[bl * size:(bl + 1) * size]
                    )

            @pl.when(turn == 0)
            def _():
                reduce_far(kc)
                if kc < 2:
                    forward(kc + 1)
                    send_tokens(kc + 2)

            return 0

        lax.fori_loop(0, 2, matrix, 0)

    def halves(kc):
        start, half = STARTS[kc], SIZES[kc] // 2
        return pl.ds(start, half), pl.ds(start + half, half), pl.ds(start // 2, half)

    def reduce_far(kc):
        rows = rows_of(kc)
        first, second, packed = halves(kc)
        a_s[rows] = part[xo, rows].astype(BF16)
        send(a_s.at[first], a_r.at[0, packed], a_send, a_recv.at[kc, 0],
             device(xp, y, z, core))
        send(a_s.at[second], a_r.at[1, packed], a_send, a_recv.at[kc, 1],
             device(xm1, y, z, core))

    def near_plain(kc):
        first, second, _ = halves(kc)
        for way, x_to, plain in ((0, xp, second), (1, xm1, first)):
            b_s[way, plain] = part[x_to, plain].astype(BF16)
            send(b_s.at[way, plain], b_r.at[way, plain], bb_send, bb_recv.at[kc],
                 device(x_to, y, z, core))

    def near_sum(kc):
        first, second, packed = halves(kc)
        for way, x_to, summed in ((0, xp, first), (1, xm1, second)):
            arrived(a_r.at[way, packed], a_recv.at[kc, way])
            b_s[way, summed] = (
                part[x_to, summed] + a_r[way, packed].astype(F32)
            ).astype(BF16)
            send(b_s.at[way, summed], b_r.at[way, summed], bb_send, bb_recv.at[kc],
                 device(x_to, y, z, core))

    def reduce_own(kc):
        rows = rows_of(kc)
        arrived(b_r.at[:, rows], bb_recv.at[kc])
        for zt in range(NZ):
            cols = slice(zt * 128, (zt + 1) * 128)
            z_s[zt, rows] = (
                part[x, rows, cols]
                + b_r[0, rows, cols].astype(F32)
                + b_r[1, rows, cols].astype(F32)
            ).astype(BF16)
        for step in FAR_FIRST:
            zt = ring(z, step, NZ)
            send(z_s.at[zt, rows], z_r.at[step - 1, rows], zz_send,
                 zz_recv.at[kc], device(x, y, zt, core))

    def reduce_z(kc):
        rows = rows_of(kc)
        arrived(z_r.at[:, rows], zz_recv.at[kc])
        total = z_s[z, rows].astype(F32)
        for i in range(NZ - 1):
            total = total + z_r[i, rows].astype(F32)
        g_full[core, rows] = total.astype(BF16)
        send(g_full.at[core, rows], g_full.at[core, rows], g_send, g_recv.at[kc],
             device(x, y, z, other))

    far = (1 - y_hi) * 2

    def right_send(_):
        loads[5].wait()
        send(rm.at[tensor], rm.at[tensor], r_send, r_recv.at[0],
             device(x, NY - 1 - y, z, core))
        send(rm.at[tensor], rm.at[tensor], r_send, r_recv.at[1],
             device(x, y, z, other))

    def right_cross(_):
        arrived(rm.at[far + core], r_recv.at[0])
        send(rm.at[far + core], rm.at[far + core], r_send, r_recv.at[2],
             device(x, y, z, other))

    def left_times(way, low, high):
        return sum(
            jnp.dot(
                lb[:, 2 * way:2 * way + 2, :, cc * HALF + low:cc * HALF + high].reshape(
                    256, high - low
                ),
                g_full[cc, low:high], preferred_element_type=F32,
            )
            for cc in range(2)
        )

    def left_most(_):
        for kc in range(4):
            arrived(g_full.at[other, rows_of(kc)], g_recv.at[kc])
        for way in range(2):
            lg_f[way] = left_times(way, 0, 384)

    def gathered(_):
        arrived(dga.at[0:2], dx_recv)

    M, B, S, C, Z = multiply, near_plain, near_sum, reduce_own, reduce_z
    F, T = forward, send_tokens
    order = (
        (gathered, 0), (M, 0), (B, 0), (left_step, 3), (S, 0),
        (M, 1), (B, 1), (left_step, 4), (S, 1), (C, 0),
        (F, 3), (T, 4), (M, 2), (B, 2), (S, 2), (C, 1), (Z, 0),
        (F, 4), (right_send, 0), (M, 3), (B, 3), (S, 3), (C, 2), (Z, 1),
        (M, 4), (B, 4), (S, 4), (C, 3), (Z, 2), (right_cross, 0),
        (C, 4), (Z, 3), (left_most, 0), (Z, 4),
    )
    for step, kc in order:
        step(kc)

    for kc in range(4, CHUNKS):
        arrived(g_full.at[other, rows_of(kc)], g_recv.at[kc])
    place = pl.ds(pl.multiple_of(z * 128, 128), 128)
    for way in range(2):
        some = slice(32 * way, 32 * way + 32)
        product = lg_f[way] + left_times(way, 384, HALF)
        lg_s[:, some] = product.astype(BF16).reshape(NZ, 32, 128)
        for step in FAR_FIRST:
            zt = ring(z, step, NZ)
            send(lg_s.at[zt, some], xm.at[some, place], t1_send, t1_recv.at[way],
                 device(x, y, zt, core))
        xm[some, place] = lg_s[z, some]
    arrived(rm.at[y_hi * 2 + other], r_recv.at[1])
    arrived(rm.at[far + other], r_recv.at[2])

    block = 2 * y + lax.div(x, 2)
    for xl in range(2):
        some = slice(32 * xl, 32 * xl + 32)
        arrived(lg_s.at[0:NZ - 1, some], t1_recv.at[xl])
        for yh in range(2):
            for cc in range(2):
                t = yh * 2 + cc
                result = jnp.dot(
                    xm[some], rm[:, :, t * 256:(t + 1) * 256].reshape(1024, 256),
                    preferred_element_type=F32,
                )
                first = xl * 8 + t * 2
                out_s[first:first + 2] = result.astype(BF16).reshape(2, 16, 256)
                for yl in range(2):
                    is_me = jnp.logical_and(
                        jnp.logical_and(x == 2 * core + xl, y == 2 * yh + yl), core == cc
                    )
                    send_or_copy(is_me, out_s.at[first + yl], out_ref.at[mine, block],
                                 t2_send, t2_recv, device(2 * core + xl, 2 * yh + yl, z, cc))

    sent(tt.at[0:3], tk_send)
    sent(tt.at[3, 0], tk_send)
    sent(fw, tf_send)
    sent(dga.at[0], dg_send)
    sent(dga.at[0, 0], dg_send)
    sent(dga.at[0:2], dx_send)
    sent(a_s, a_send)
    sent(b_s, bb_send)
    sent(z_s.at[0:NZ - 1], zz_send)
    sent(g_full.at[0], g_send)
    sent(lb.at[0:NZ - 1], l3_send)
    sent(rm.at[0:3], r_send)
    sent(lg_s.at[0:NZ - 1], t1_send)
    sent(l1.at[0:3], l1_send)
    pl.when(jnp.logical_not(jnp.logical_and(y == y_t, core == l_core)))(
        lambda: sent(l1.at[3], l1_send)
    )
    arrived(out_ref, t2_recv)
    sent(out_s.at[0:15], t2_send)
    pl.when(core != l_core)(lambda: sent(out_s.at[15], t2_send))


def local(tokens, gate_pre, up_pre, d_hidden, left_roots, right_roots):
    dma = pltpu.SemaphoreType.DMA
    vm = pltpu.VMEM
    scratch = [
        vm((128, 8192), BF16), vm((512, 256), BF16), vm((512, 256), BF16),
        vm((512, 256), BF16), vm((16, 2, 2, 1024), BF16),
        vm((4, 2, 2, 512, 256), BF16),
        vm((NY, 2, 2, HALF, 128), BF16),
        vm((2, HALF, 1024), BF16),
        vm((2, 2, HALF, 128), BF16),
        vm((4, HALF, 1024), F32),
        vm((HALF, 1024), BF16),
        vm((2, HALF // 2, 1024), BF16),
        vm((2, HALF, 1024), BF16),
        vm((2, HALF, 1024), BF16),
        vm((NZ, HALF, 128), BF16),
        vm((NZ - 1, HALF, 128), BF16),
        vm((2, HALF, 128), BF16),
        vm((4, 16, 1024), BF16),
        vm((NZ, 4, 16, 1024), BF16),
        vm((2, 256, 128), F32),
        vm((NZ, 64, 128), BF16),
        vm((64, 1024), BF16),
        vm((4, 256, 1024), BF16),
        vm((16, 16, 256), BF16),
        dma, dma((6,)), dma, dma,
        dma, dma((CHUNKS,)), dma,
        dma((CHUNKS, 2)),
        dma, dma((CHUNKS, 2)), dma, dma((CHUNKS,)),
        dma, dma((CHUNKS,)), dma, dma((CHUNKS,)),
        dma, dma, dma, dma((NZ - 1,)), dma, dma((3,)),
        dma, dma((2,)), dma, dma, dma((6,)),
    ]
    out = pl.pallas_call(
        kernel,
        out_shape=jax.ShapeDtypeStruct((2, 8, 16, 256), BF16),
        in_specs=[pl.BlockSpec(memory_space=pltpu.HBM)] * 6,
        out_specs=pl.BlockSpec(memory_space=pltpu.VMEM),
        scratch_shapes=scratch,
        compiler_params=pltpu.CompilerParams(
            collective_id=0, has_side_effects=True, vmem_limit_bytes=60 * 1024 * 1024
        ),
        cost_estimate=pl.CostEstimate(
            flops=4_500_000_000, bytes_accessed=8_000_000, transcendentals=131072
        ),
    )(tokens, gate_pre, up_pre, d_hidden, left_roots, right_roots)
    return out.transpose(2, 1, 0, 3).astype(F32)


def solution(mesh):
    in_specs = (
        P(("dp", "tensor"), None),
        P("dp", "tensor"),
        P("dp", "tensor"),
        P("dp", "tensor"),
        P("dp", None, None, None),
        P(None, "tensor", None),
    )
    out_specs = P("dp", None, None, "tensor")
    return jax.shard_map(local, mesh=mesh, in_specs=in_specs, out_specs=out_specs, check_vma=False)
```

```python
import jax
import jax.numpy as jnp
from jax import lax
from jax.experimental import pallas as pl
from jax.experimental.pallas import tpu as pltpu
from jax.sharding import PartitionSpec as P

MESH = pl.DeviceIdType.MESH
F32 = jnp.float32
BF16 = jnp.bfloat16

NX, NY, NZ = 4, 4, 8
SIZES = (96, 128, 128, 96, 64)
STARTS = tuple(sum(SIZES[:i]) for i in range(len(SIZES)))
CHUNKS = len(SIZES)
HALF = 512
FAR_FIRST = (4, 3, 5, 2, 6, 1, 7)


def device(x, y, z, core):
    return ((x * NZ + z) * 2 + lax.rem(y, 2), lax.div(y, 2) * 2 + core)


def ring(value, step, size):
    return lax.rem(value + (step + size), size)


def lane_of(y, core):
    return pl.multiple_of(
        lax.rem(y, 2) * 512 + (lax.div(y, 2) * 2 + core) * 128, 128
    )


def kernel(
    tok_hbm, gate_hbm, up_hbm, dh_hbm, left_hbm, right_hbm, out_ref,
    tok_ref, gate_ref, up_ref, dh_ref, left_ref, dga, tt, tk, fw, part, a_s, a_r, b_s, b_r, z_s, z_r, g_full,
    l1, lb, lg_f, lg_s, xm, rm, out_s,
    dg_send, dg_recv, dx_send, dx_recv, tk_send, tk_recv, tf_send,
    fw_recv, a_send, a_recv, bb_send, bb_recv, zz_send, zz_recv,
    g_send, g_recv, l1_send, l1_recv, l3_send, l3_recv, r_send, r_recv,
    t1_send, t1_recv, t2_send, t2_recv, in_sem,
):
    dp = lax.axis_index("dp")
    tensor = lax.axis_index("tensor")
    y_lo = lax.rem(dp, 2)
    z = lax.rem(lax.div(dp, 2), NZ)
    x = lax.div(dp, 2 * NZ)
    y_hi = lax.div(tensor, 2)
    core = lax.rem(tensor, 2)
    y = y_hi * 2 + y_lo
    other = 1 - core
    xp, xm1, xo = ring(x, 1, NX), ring(x, -1, NX), ring(x, 2, NX)
    yp, ym, yo = ring(y, 1, NY), ring(y, -1, NY), ring(y, 2, NY)

    def send(src, dst, ssem, rsem, dev):
        pltpu.make_async_remote_copy(
            src_ref=src, dst_ref=dst, send_sem=ssem, recv_sem=rsem,
            device_id=dev, device_id_type=MESH,
        ).start()

    def send_or_copy(is_me, src, dst, ssem, rsem, dev):
        @pl.when(is_me)
        def _():
            pltpu.make_async_copy(src, dst, rsem).start()

        @pl.when(jnp.logical_not(is_me))
        def _():
            send(src, dst, ssem, rsem, dev)

    def arrived(dst, rsem):
        pltpu.make_async_remote_copy(
            src_ref=dst, dst_ref=dst, send_sem=rsem, recv_sem=rsem,
            device_id=device(x, y, z, other), device_id_type=MESH,
        ).wait_recv()

    def sent(src, ssem):
        pltpu.make_async_remote_copy(
            src_ref=src, dst_ref=src, send_sem=ssem, recv_sem=ssem,
            device_id=device(x, y, z, other), device_id_type=MESH,
        ).wait_send()

    y_t = y_hi * 2 + core
    mine = lax.rem(x, 2)
    loads = [
        pltpu.make_async_copy(src, dst, in_sem.at[i])
        for i, (src, dst) in enumerate((
            (gate_hbm, gate_ref), (up_hbm, up_ref), (dh_hbm, dh_ref),
            (left_hbm.at[:, pl.ds(2 * y_t, 2)], left_ref), (tok_hbm, tok_ref),
            (right_hbm.at[mine], rm.at[tensor]),
        ))
    ]
    for load in loads:
        load.start()

    barrier = pltpu.get_barrier_semaphore()
    partners = []
    for step_x in range(NX):
        for step_y in range(NY):
            for cc in range(2):
                if step_x or step_y or cc:
                    partners.append(device(
                        ring(x, step_x, NX), ring(y, step_y, NY), z, lax.rem(core + cc, 2)
                    ))
    for step in range(1, NZ):
        partners.append(device(x, y, ring(z, step, NZ), core))
    for partner in partners:
        pl.semaphore_signal(barrier, inc=1, device_id=partner, device_id_type=MESH)

    def elementwise(i, _):
        rows = pl.ds(pl.multiple_of(i * 64, 64), 64)
        g = gate_ref[rows, :].astype(F32)
        u = up_ref[rows, :].astype(F32)
        h = dh_ref[rows, :].astype(F32)
        s = 1.0 / (1.0 + jnp.exp(-g))
        dga[tensor, 0, y_lo, rows, :] = (h * u * s * (1.0 + g * (1.0 - s))).astype(BF16)
        dga[tensor, 1, y_lo, rows, :] = (h * g * s).astype(BF16)
        return 0

    for load in loads[:3]:
        load.wait()
    lax.fori_loop(0, 8, elementwise, 0)
    pl.semaphore_wait(barrier, len(partners))

    def dg(y_from, m):
        return dga.at[lax.div(y_from, 2) * 2 + core, m, lax.rem(y_from, 2)]

    def along(y_from, m, index, y_to):
        send(dg(y_from, m), dg(y_from, m), dg_send, dg_recv.at[index], device(x, y_to, z, core))

    def cross(y_from, m):
        send(dg(y_from, m), dg(y_from, m), dx_send, dx_recv, device(x, y, z, other))

    along(y, 0, 0, yp)
    along(y, 1, 1, ym)
    along(y, 1, 2, yp)
    along(y, 0, 3, ym)
    cross(y, 0)
    cross(y, 1)

    loads[3].wait()
    l_core = lax.div(x, 2)
    l_slot = lax.rem(x, 2) * 2 + y_lo
    for x_t in range(NX):
        is_me = jnp.logical_and(jnp.logical_and(x == x_t, y == y_t), core == l_core)
        l1[x_t] = left_ref[:, x_t // 2, x_t % 2]
        send_or_copy(is_me, l1.at[x_t], lb.at[z, l_slot], l1_send, l1_recv,
                     device(x_t, y_t, z, l_core))

    loads[4].wait()

    def transpose(y_to, _):
        for bl in range(2):
            for cc in range(2):
                for part_of in range(4):
                    column = pl.multiple_of(
                        y_to * 2048 + (bl * 1024 + cc * 512 + part_of * 128), 128
                    )
                    tt[y_to, bl, cc, part_of * 128:(part_of + 1) * 128] = (
                        tok_ref[:, pl.ds(column, 128)].T
                    )
        return 0

    lax.fori_loop(0, NY, transpose, 0)

    def rows_of(kc):
        return pl.ds(STARTS[kc], SIZES[kc])

    def send_tokens(kc):
        rows = rows_of(kc)
        here = tk.at[:, rows, pl.ds(lane_of(y, core), 128)]
        send(tt.at[yo, 0, :, rows], fw.at[0, :, rows], tk_send, fw_recv.at[kc, 0],
             device(x, yp, z, core))
        send(tt.at[yo, 1, :, rows], fw.at[1, :, rows], tk_send, fw_recv.at[kc, 1],
             device(x, ym, z, core))
        for cc in range(2):
            send(tt.at[yp, :, cc, rows], here, tk_send, tk_recv.at[kc], device(x, yp, z, cc))
            send(tt.at[ym, :, cc, rows], here, tk_send, tk_recv.at[kc], device(x, ym, z, cc))
        send(tt.at[y, :, other, rows], here, tk_send, tk_recv.at[kc], device(x, y, z, other))
        pltpu.make_async_copy(tt.at[y, :, core, rows], here, tk_recv.at[kc]).start()

    def forward(kc):
        rows = rows_of(kc)
        for way, y_from, y_to in ((0, ym, yp), (1, yp, ym)):
            arrived(fw.at[way, :, rows], fw_recv.at[kc, way])
            there = tk.at[way, rows, pl.ds(lane_of(y_from, core), 128)]
            for cc in range(2):
                send(fw.at[way, cc, rows], there, tf_send, tk_recv.at[kc],
                     device(x, y_to, z, cc))

    arrived(dg(ym, 0), dg_recv.at[0])
    along(ym, 0, 4, yp)
    arrived(dg(yp, 1), dg_recv.at[1])
    along(yp, 1, 5, ym)
    cross(ym, 0)
    cross(yp, 1)

    zp, zm = ring(z, 1, NZ), ring(z, -1, NZ)

    def left_up(step):
        slot = ring(z, -step, NZ)
        if step > 0:
            arrived(lb.at[slot], l3_recv.at[step - 1])
        if step < 4:
            send(lb.at[slot], lb.at[slot], l3_send, l3_recv.at[step],
                 device(x, y, zp, core))

    def left_down(step):
        slot = ring(z, step, NZ)
        if step > 0:
            arrived(lb.at[slot], l3_recv.at[3 + step])
        if step < 3:
            send(lb.at[slot], lb.at[slot], l3_send, l3_recv.at[4 + step],
                 device(x, y, zm, core))

    def left_step(step):
        left_up(step)
        if step < 4:
            left_down(step)

    send_tokens(0)
    arrived(lb.at[z], l1_recv)
    left_step(0)
    arrived(dg(ym, 1), dg_recv.at[2])
    cross(ym, 1)
    arrived(dg(yp, 0), dg_recv.at[3])
    cross(yp, 0)
    left_step(1)

    arrived(dg(yo, 0), dg_recv.at[4])
    cross(yo, 0)
    arrived(dg(yo, 1), dg_recv.at[5])
    cross(yo, 1)
    forward(0)
    send_tokens(1)
    left_step(2)

    def multiply(kc):
        rows, size = rows_of(kc), SIZES[kc]
        arrived(tk.at[:, rows], tk_recv.at[kc])

        def matrix(turn, _):
            m = lax.rem(mine + turn, 2)
            for t in range(4):
                total = jnp.dot(
                    tk[:, rows].reshape(2 * size, 1024), dga[t, m].reshape(1024, 256),
                    preferred_element_type=F32,
                )
                for bl in range(2):
                    part[bl * 2 + m, rows, t * 256:(t + 1) * 256] = (
                        total[bl * size:(bl + 1) * size]
                    )

            @pl.when(turn == 0)
            def _():
                reduce_far(kc)
                if kc < 2:
                    forward(kc + 1)
                    send_tokens(kc + 2)

            return 0

        lax.fori_loop(0, 2, matrix, 0)

    def halves(kc):
        start, half = STARTS[kc], SIZES[kc] // 2
        return pl.ds(start, half), pl.ds(start + half, half), pl.ds(start // 2, half)

    def reduce_far(kc):
        rows = rows_of(kc)
        first, second, packed = halves(kc)
        a_s[rows] = part[xo, rows].astype(BF16)
        send(a_s.at[first], a_r.at[0, packed], a_send, a_recv.at[kc, 0],
             device(xp, y, z, core))
        send(a_s.at[second], a_r.at[1, packed], a_send, a_recv.at[kc, 1],
             device(xm1, y, z, core))

    def near_plain(kc):
        first, second, _ = halves(kc)
        for way, x_to, plain in ((0, xp, second), (1, xm1, first)):
            b_s[way, plain] = part[x_to, plain].astype(BF16)
            send(b_s.at[way, plain], b_r.at[way, plain], bb_send, bb_recv.at[kc],
                 device(x_to, y, z, core))

    def near_sum(kc):
        first, second, packed = halves(kc)
        for way, x_to, summed in ((0, xp, first), (1, xm1, second)):
            arrived(a_r.at[way, packed], a_recv.at[kc, way])
            b_s[way, summed] = (
                part[x_to, summed] + a_r[way, packed].astype(F32)
            ).astype(BF16)
            send(b_s.at[way, summed], b_r.at[way, summed], bb_send, bb_recv.at[kc],
                 device(x_to, y, z, core))

    def reduce_own(kc):
        rows = rows_of(kc)
        arrived(b_r.at[:, rows], bb_recv.at[kc])
        for zt in range(NZ):
            cols = slice(zt * 128, (zt + 1) * 128)
            z_s[zt, rows] = (
                part[x, rows, cols]
                + b_r[0, rows, cols].astype(F32)
                + b_r[1, rows, cols].astype(F32)
            ).astype(BF16)
        for step in FAR_FIRST:
            zt = ring(z, step, NZ)
            send(z_s.at[zt, rows], z_r.at[step - 1, rows], zz_send,
                 zz_recv.at[kc], device(x, y, zt, core))

    def reduce_z(kc):
        rows = rows_of(kc)
        arrived(z_r.at[:, rows], zz_recv.at[kc])
        total = z_s[z, rows].astype(F32)
        for i in range(NZ - 1):
            total = total + z_r[i, rows].astype(F32)
        g_full[core, rows] = total.astype(BF16)
        send(g_full.at[core, rows], g_full.at[core, rows], g_send, g_recv.at[kc],
             device(x, y, z, other))

    far = (1 - y_hi) * 2

    def right_send(_):
        loads[5].wait()
        send(rm.at[tensor], rm.at[tensor], r_send, r_recv.at[0],
             device(x, NY - 1 - y, z, core))
        send(rm.at[tensor], rm.at[tensor], r_send, r_recv.at[1],
             device(x, y, z, other))

    def right_cross(_):
        arrived(rm.at[far + core], r_recv.at[0])
        send(rm.at[far + core], rm.at[far + core], r_send, r_recv.at[2],
             device(x, y, z, other))

    def left_times(way, low, high):
        return sum(
            jnp.dot(
                lb[:, 2 * way:2 * way + 2, :, cc * HALF + low:cc * HALF + high].reshape(
                    256, high - low
                ),
                g_full[cc, low:high], preferred_element_type=F32,
            )
            for cc in range(2)
        )

    def left_most(_):
        for kc in range(4):
            arrived(g_full.at[other, rows_of(kc)], g_recv.at[kc])
        for way in range(2):
            lg_f[way] = left_times(way, 0, 384)

    def gathered(_):
        arrived(dga.at[0:2], dx_recv)

    M, B, S, C, Z = multiply, near_plain, near_sum, reduce_own, reduce_z
    F, T = forward, send_tokens
    order = (
        (gathered, 0), (M, 0), (B, 0), (left_step, 3), (S, 0),
        (M, 1), (B, 1), (left_step, 4), (S, 1), (C, 0),
        (F, 3), (T, 4), (M, 2), (B, 2), (S, 2), (C, 1), (Z, 0),
        (F, 4), (right_send, 0), (M, 3), (B, 3), (S, 3), (C, 2), (Z, 1),
        (M, 4), (B, 4), (S, 4), (C, 3), (Z, 2), (right_cross, 0),
        (C, 4), (Z, 3), (left_most, 0), (Z, 4),
    )
    for step, kc in order:
        step(kc)

    for kc in range(4, CHUNKS):
        arrived(g_full.at[other, rows_of(kc)], g_recv.at[kc])
    place = pl.ds(pl.multiple_of(z * 128, 128), 128)
    for way in range(2):
        some = slice(32 * way, 32 * way + 32)
        product = lg_f[way] + left_times(way, 384, HALF)
        lg_s[:, some] = product.astype(BF16).reshape(NZ, 32, 128)
        for step in FAR_FIRST:
            zt = ring(z, step, NZ)
            send(lg_s.at[zt, some], xm.at[some, place], t1_send, t1_recv.at[way],
                 device(x, y, zt, core))
        xm[some, place] = lg_s[z, some]
    arrived(rm.at[y_hi * 2 + other], r_recv.at[1])
    arrived(rm.at[far + other], r_recv.at[2])

    block = 2 * y + lax.div(x, 2)
    for xl in range(2):
        some = slice(32 * xl, 32 * xl + 32)
        arrived(lg_s.at[0:NZ - 1, some], t1_recv.at[xl])
        for yh in range(2):
            for cc in range(2):
                t = yh * 2 + cc
                result = jnp.dot(
                    xm[some], rm[:, :, t * 256:(t + 1) * 256].reshape(1024, 256),
                    preferred_element_type=F32,
                )
                first = xl * 8 + t * 2
                out_s[first:first + 2] = result.reshape(2, 16, 256)
                for yl in range(2):
                    is_me = jnp.logical_and(
                        jnp.logical_and(x == 2 * core + xl, y == 2 * yh + yl), core == cc
                    )
                    send_or_copy(is_me, out_s.at[first + yl], out_ref.at[mine, block],
                                 t2_send, t2_recv, device(2 * core + xl, 2 * yh + yl, z, cc))

    sent(tt.at[0:3], tk_send)
    sent(tt.at[3, 0], tk_send)
    sent(fw, tf_send)
    sent(dga.at[0], dg_send)
    sent(dga.at[0, 0], dg_send)
    sent(dga.at[0:2], dx_send)
    sent(a_s, a_send)
    sent(b_s, bb_send)
    sent(z_s.at[0:NZ - 1], zz_send)
    sent(g_full.at[0], g_send)
    sent(lb.at[0:NZ - 1], l3_send)
    sent(rm.at[0:3], r_send)
    sent(lg_s.at[0:NZ - 1], t1_send)
    sent(l1.at[0:3], l1_send)
    pl.when(jnp.logical_not(jnp.logical_and(y == y_t, core == l_core)))(
        lambda: sent(l1.at[3], l1_send)
    )
    arrived(out_ref, t2_recv)
    sent(out_s.at[0:15], t2_send)
    pl.when(core != l_core)(lambda: sent(out_s.at[15], t2_send))


def local(tokens, gate_pre, up_pre, d_hidden, left_roots, right_roots):
    dma = pltpu.SemaphoreType.DMA
    vm = pltpu.VMEM
    scratch = [
        vm((128, 8192), BF16), vm((512, 256), BF16), vm((512, 256), BF16),
        vm((512, 256), BF16), vm((16, 2, 2, 1024), BF16),
        vm((4, 2, 2, 512, 256), BF16),
        vm((NY, 2, 2, HALF, 128), BF16),
        vm((2, HALF, 1024), BF16),
        vm((2, 2, HALF, 128), BF16),
        vm((4, HALF, 1024), F32),
        vm((HALF, 1024), BF16),
        vm((2, HALF // 2, 1024), BF16),
        vm((2, HALF, 1024), BF16),
        vm((2, HALF, 1024), BF16),
        vm((NZ, HALF, 128), BF16),
        vm((NZ - 1, HALF, 128), BF16),
        vm((2, HALF, 128), BF16),
        vm((4, 16, 1024), BF16),
        vm((NZ, 4, 16, 1024), BF16),
        vm((2, 256, 128), F32),
        vm((NZ, 64, 128), BF16),
        vm((64, 1024), BF16),
        vm((4, 256, 1024), BF16),
        vm((16, 16, 256), F32),
        dma, dma((6,)), dma, dma,
        dma, dma((CHUNKS,)), dma,
        dma((CHUNKS, 2)),
        dma, dma((CHUNKS, 2)), dma, dma((CHUNKS,)),
        dma, dma((CHUNKS,)), dma, dma((CHUNKS,)),
        dma, dma, dma, dma((NZ - 1,)), dma, dma((3,)),
        dma, dma((2,)), dma, dma, dma((6,)),
    ]
    out = pl.pallas_call(
        kernel,
        out_shape=jax.ShapeDtypeStruct((2, 8, 16, 256), F32),
        in_specs=[pl.BlockSpec(memory_space=pltpu.HBM)] * 6,
        out_specs=pl.BlockSpec(memory_space=pltpu.VMEM),
        scratch_shapes=scratch,
        compiler_params=pltpu.CompilerParams(
            collective_id=0, has_side_effects=True, vmem_limit_bytes=60 * 1024 * 1024
        ),
        cost_estimate=pl.CostEstimate(
            flops=4_500_000_000, bytes_accessed=8_000_000, transcendentals=131072
        ),
    )(tokens, gate_pre, up_pre, d_hidden, left_roots, right_roots)
    return out.transpose(2, 1, 0, 3)


def solution(mesh):
    in_specs = (
        P(("dp", "tensor"), None),
        P("dp", "tensor"),
        P("dp", "tensor"),
        P("dp", "tensor"),
        P("dp", None, None, None),
        P(None, "tensor", None),
    )
    out_specs = P("dp", None, None, "tensor")
    return jax.shard_map(local, mesh=mesh, in_specs=in_specs, out_specs=out_specs, check_vma=False)
```

```python
import jax
import jax.numpy as jnp
from jax import lax
from jax.experimental import pallas as pl
from jax.experimental.pallas import tpu as pltpu
from jax.sharding import PartitionSpec as P

MESH = pl.DeviceIdType.MESH
F32 = jnp.float32
BF16 = jnp.bfloat16

NX, NY, NZ = 4, 4, 8
SIZES = (96, 128, 128, 96, 64)
STARTS = tuple(sum(SIZES[:i]) for i in range(len(SIZES)))
CHUNKS = len(SIZES)
HALF = 512
FAR_FIRST = (4, 3, 5, 2, 6, 1, 7)


def device(x, y, z, core):
    return ((x * NZ + z) * 2 + lax.rem(y, 2), lax.div(y, 2) * 2 + core)


def ring(value, step, size):
    return lax.rem(value + (step + size), size)


def lane_of(y, core):
    return pl.multiple_of(
        lax.rem(y, 2) * 512 + (lax.div(y, 2) * 2 + core) * 128, 128
    )


def kernel(
    tok_hbm, gate_hbm, up_hbm, dh_hbm, left_hbm, right_hbm, out_ref,
    tok_ref, gate_ref, up_ref, dh_ref, left_ref, dga, tt, tk, fw, part, a_s, a_r, b_s, b_r, z_s, z_r, z_q, g_full,
    l1, lb, lg_f, lg_s, xm, rm, out_s,
    dg_send, dg_recv, dx_send, dx_recv, tk_send, tk_recv, tf_send,
    fw_recv, a_send, a_recv, bb_send, bb_recv, zz_send, zz_recv, zq_recv,
    g_send, g_recv, l1_send, l1_recv, l3_send, l3_recv, r_send, r_recv,
    t1_send, t1_recv, t2_send, t2_recv, in_sem,
):
    dp = lax.axis_index("dp")
    tensor = lax.axis_index("tensor")
    y_lo = lax.rem(dp, 2)
    z = lax.rem(lax.div(dp, 2), NZ)
    x = lax.div(dp, 2 * NZ)
    y_hi = lax.div(tensor, 2)
    core = lax.rem(tensor, 2)
    y = y_hi * 2 + y_lo
    other = 1 - core
    xp, xm1, xo = ring(x, 1, NX), ring(x, -1, NX), ring(x, 2, NX)
    yp, ym, yo = ring(y, 1, NY), ring(y, -1, NY), ring(y, 2, NY)

    def send(src, dst, ssem, rsem, dev):
        pltpu.make_async_remote_copy(
            src_ref=src, dst_ref=dst, send_sem=ssem, recv_sem=rsem,
            device_id=dev, device_id_type=MESH,
        ).start()

    def send_or_copy(is_me, src, dst, ssem, rsem, dev):
        @pl.when(is_me)
        def _():
            pltpu.make_async_copy(src, dst, rsem).start()

        @pl.when(jnp.logical_not(is_me))
        def _():
            send(src, dst, ssem, rsem, dev)

    def arrived(dst, rsem):
        pltpu.make_async_remote_copy(
            src_ref=dst, dst_ref=dst, send_sem=rsem, recv_sem=rsem,
            device_id=device(x, y, z, other), device_id_type=MESH,
        ).wait_recv()

    def sent(src, ssem):
        pltpu.make_async_remote_copy(
            src_ref=src, dst_ref=src, send_sem=ssem, recv_sem=ssem,
            device_id=device(x, y, z, other), device_id_type=MESH,
        ).wait_send()

    y_t = y_hi * 2 + core
    mine = lax.rem(x, 2)
    loads = [
        pltpu.make_async_copy(src, dst, in_sem.at[i])
        for i, (src, dst) in enumerate((
            (gate_hbm, gate_ref), (up_hbm, up_ref), (dh_hbm, dh_ref),
            (left_hbm.at[:, pl.ds(2 * y_t, 2)], left_ref), (tok_hbm, tok_ref),
            (right_hbm.at[mine], rm.at[tensor]),
        ))
    ]
    for load in loads:
        load.start()

    barrier = pltpu.get_barrier_semaphore()
    partners = []
    for step_x in range(NX):
        for step_y in range(NY):
            for cc in range(2):
                if step_x or step_y or cc:
                    partners.append(device(
                        ring(x, step_x, NX), ring(y, step_y, NY), z, lax.rem(core + cc, 2)
                    ))
    for step in range(1, NZ):
        partners.append(device(x, y, ring(z, step, NZ), core))
    for partner in partners:
        pl.semaphore_signal(barrier, inc=1, device_id=partner, device_id_type=MESH)

    def elementwise(i, _):
        rows = pl.ds(pl.multiple_of(i * 64, 64), 64)
        g = gate_ref[rows, :].astype(F32)
        u = up_ref[rows, :].astype(F32)
        h = dh_ref[rows, :].astype(F32)
        s = 1.0 / (1.0 + jnp.exp(-g))
        dga[tensor, 0, y_lo, rows, :] = (h * u * s * (1.0 + g * (1.0 - s))).astype(BF16)
        dga[tensor, 1, y_lo, rows, :] = (h * g * s).astype(BF16)
        return 0

    for load in loads[:3]:
        load.wait()
    lax.fori_loop(0, 8, elementwise, 0)
    pl.semaphore_wait(barrier, len(partners))

    def dg(y_from, m):
        return dga.at[lax.div(y_from, 2) * 2 + core, m, lax.rem(y_from, 2)]

    def along(y_from, m, index, y_to):
        send(dg(y_from, m), dg(y_from, m), dg_send, dg_recv.at[index], device(x, y_to, z, core))

    def cross(y_from, m):
        send(dg(y_from, m), dg(y_from, m), dx_send, dx_recv, device(x, y, z, other))

    along(y, 0, 0, yp)
    along(y, 1, 1, ym)
    along(y, 1, 2, yp)
    along(y, 0, 3, ym)
    cross(y, 0)
    cross(y, 1)

    loads[3].wait()
    l_core = lax.div(x, 2)
    l_slot = lax.rem(x, 2) * 2 + y_lo
    for x_t in range(NX):
        is_me = jnp.logical_and(jnp.logical_and(x == x_t, y == y_t), core == l_core)
        l1[x_t] = left_ref[:, x_t // 2, x_t % 2]
        send_or_copy(is_me, l1.at[x_t], lb.at[z, l_slot], l1_send, l1_recv,
                     device(x_t, y_t, z, l_core))

    loads[4].wait()

    def transpose(y_to, _):
        for bl in range(2):
            for cc in range(2):
                for part_of in range(4):
                    column = pl.multiple_of(
                        y_to * 2048 + (bl * 1024 + cc * 512 + part_of * 128), 128
                    )
                    tt[y_to, bl, cc, part_of * 128:(part_of + 1) * 128] = (
                        tok_ref[:, pl.ds(column, 128)].T
                    )
        return 0

    lax.fori_loop(0, NY, transpose, 0)

    def rows_of(kc):
        return pl.ds(STARTS[kc], SIZES[kc])

    def send_tokens(kc):
        rows = rows_of(kc)
        here = tk.at[:, rows, pl.ds(lane_of(y, core), 128)]
        send(tt.at[yo, 0, :, rows], fw.at[0, :, rows], tk_send, fw_recv.at[kc, 0],
             device(x, yp, z, core))
        send(tt.at[yo, 1, :, rows], fw.at[1, :, rows], tk_send, fw_recv.at[kc, 1],
             device(x, ym, z, core))
        for cc in range(2):
            send(tt.at[yp, :, cc, rows], here, tk_send, tk_recv.at[kc], device(x, yp, z, cc))
            send(tt.at[ym, :, cc, rows], here, tk_send, tk_recv.at[kc], device(x, ym, z, cc))
        send(tt.at[y, :, other, rows], here, tk_send, tk_recv.at[kc], device(x, y, z, other))
        pltpu.make_async_copy(tt.at[y, :, core, rows], here, tk_recv.at[kc]).start()

    def forward(kc):
        rows = rows_of(kc)
        for way, y_from, y_to in ((0, ym, yp), (1, yp, ym)):
            arrived(fw.at[way, :, rows], fw_recv.at[kc, way])
            there = tk.at[way, rows, pl.ds(lane_of(y_from, core), 128)]
            for cc in range(2):
                send(fw.at[way, cc, rows], there, tf_send, tk_recv.at[kc],
                     device(x, y_to, z, cc))

    arrived(dg(ym, 0), dg_recv.at[0])
    along(ym, 0, 4, yp)
    arrived(dg(yp, 1), dg_recv.at[1])
    along(yp, 1, 5, ym)
    cross(ym, 0)
    cross(yp, 1)

    zp, zm = ring(z, 1, NZ), ring(z, -1, NZ)

    def left_up(step):
        slot = ring(z, -step, NZ)
        if step > 0:
            arrived(lb.at[slot], l3_recv.at[step - 1])
        if step < 4:
            send(lb.at[slot], lb.at[slot], l3_send, l3_recv.at[step],
                 device(x, y, zp, core))

    def left_down(step):
        slot = ring(z, step, NZ)
        if step > 0:
            arrived(lb.at[slot], l3_recv.at[3 + step])
        if step < 3:
            send(lb.at[slot], lb.at[slot], l3_send, l3_recv.at[4 + step],
                 device(x, y, zm, core))

    def left_step(step):
        left_up(step)
        if step < 4:
            left_down(step)

    send_tokens(0)
    arrived(lb.at[z], l1_recv)
    left_step(0)
    arrived(dg(ym, 1), dg_recv.at[2])
    cross(ym, 1)
    arrived(dg(yp, 0), dg_recv.at[3])
    cross(yp, 0)
    left_step(1)

    arrived(dg(yo, 0), dg_recv.at[4])
    cross(yo, 0)
    arrived(dg(yo, 1), dg_recv.at[5])
    cross(yo, 1)
    forward(0)
    send_tokens(1)
    left_step(2)

    def multiply(kc):
        rows, size = rows_of(kc), SIZES[kc]
        arrived(tk.at[:, rows], tk_recv.at[kc])

        def matrix(turn, _):
            m = lax.rem(mine + turn, 2)
            for t in range(4):
                total = jnp.dot(
                    tk[:, rows].reshape(2 * size, 1024), dga[t, m].reshape(1024, 256),
                    preferred_element_type=F32,
                )
                for bl in range(2):
                    part[bl * 2 + m, rows, t * 256:(t + 1) * 256] = (
                        total[bl * size:(bl + 1) * size]
                    )

            @pl.when(turn == 0)
            def _():
                reduce_far(kc)
                if kc < 2:
                    forward(kc + 1)
                    send_tokens(kc + 2)

            return 0

        lax.fori_loop(0, 2, matrix, 0)

    def halves(kc):
        start, half = STARTS[kc], SIZES[kc] // 2
        return pl.ds(start, half), pl.ds(start + half, half), pl.ds(start // 2, half)

    def reduce_far(kc):
        rows = rows_of(kc)
        first, second, packed = halves(kc)
        a_s[rows] = part[xo, rows].astype(BF16)
        send(a_s.at[first], a_r.at[0, packed], a_send, a_recv.at[kc, 0],
             device(xp, y, z, core))
        send(a_s.at[second], a_r.at[1, packed], a_send, a_recv.at[kc, 1],
             device(xm1, y, z, core))

    def near_plain(kc):
        first, second, _ = halves(kc)
        for way, x_to, plain in ((0, xp, second), (1, xm1, first)):
            b_s[way, plain] = part[x_to, plain].astype(BF16)
            send(b_s.at[way, plain], b_r.at[way, plain], bb_send, bb_recv.at[kc],
                 device(x_to, y, z, core))

    def near_sum(kc):
        first, second, packed = halves(kc)
        for way, x_to, summed in ((0, xp, first), (1, xm1, second)):
            arrived(a_r.at[way, packed], a_recv.at[kc, way])
            b_s[way, summed] = (
                part[x_to, summed] + a_r[way, packed].astype(F32)
            ).astype(BF16)
            send(b_s.at[way, summed], b_r.at[way, summed], bb_send, bb_recv.at[kc],
                 device(x_to, y, z, core))

    def reduce_own(kc):
        rows = rows_of(kc)
        arrived(b_r.at[:, rows], bb_recv.at[kc])
        for zt in range(NZ):
            cols = slice(zt * 128, (zt + 1) * 128)
            z_s[zt, rows] = (
                part[x, rows, cols]
                + b_r[0, rows, cols].astype(F32)
                + b_r[1, rows, cols].astype(F32)
            ).astype(BF16)
        steps = FAR_FIRST
        if kc < CHUNKS - 1:
            far_slice = z_s.at[ring(z, 4, NZ), rows]
            send(far_slice, z_q.at[rows], zz_send, zq_recv.at[kc], device(x, y, zm, core))
            steps = (3, 2, 6, 1, 7)
        for step in steps:
            zt = ring(z, step, NZ)
            send(z_s.at[zt, rows], z_r.at[step - 1, rows], zz_send,
                 zz_recv.at[kc], device(x, y, zt, core))

    def relay_z(kc):
        rows = rows_of(kc)
        zt = ring(z, 5, NZ)
        arrived(z_q.at[rows], zq_recv.at[kc])
        z_s[zt, rows] = (z_s[zt, rows].astype(F32) + z_q[rows].astype(F32)).astype(BF16)
        send(z_s.at[zt, rows], z_r.at[4, rows], zz_send, zz_recv.at[kc],
             device(x, y, zt, core))

    def reduce_z(kc):
        rows = rows_of(kc)
        slots = (0, 1, 2, 4, 5, 6) if kc < CHUNKS - 1 else range(NZ - 1)
        arrived(z_r.at[0:len(slots), rows], zz_recv.at[kc])
        total = z_s[z, rows].astype(F32)
        for i in slots:
            total = total + z_r[i, rows].astype(F32)
        g_full[core, rows] = total.astype(BF16)
        send(g_full.at[core, rows], g_full.at[core, rows], g_send, g_recv.at[kc],
             device(x, y, z, other))

    far = (1 - y_hi) * 2

    def right_send(_):
        loads[5].wait()
        send(rm.at[tensor], rm.at[tensor], r_send, r_recv.at[0],
             device(x, NY - 1 - y, z, core))
        send(rm.at[tensor], rm.at[tensor], r_send, r_recv.at[1],
             device(x, y, z, other))

    def right_cross(_):
        arrived(rm.at[far + core], r_recv.at[0])
        send(rm.at[far + core], rm.at[far + core], r_send, r_recv.at[2],
             device(x, y, z, other))

    def left_times(way, low, high):
        return sum(
            jnp.dot(
                lb[:, 2 * way:2 * way + 2, :, cc * HALF + low:cc * HALF + high].reshape(
                    256, high - low
                ),
                g_full[cc, low:high], preferred_element_type=F32,
            )
            for cc in range(2)
        )

    def left_most(_):
        for kc in range(4):
            arrived(g_full.at[other, rows_of(kc)], g_recv.at[kc])
        for way in range(2):
            lg_f[way] = left_times(way, 0, 384)

    def gathered(_):
        arrived(dga.at[0:2], dx_recv)

    M, B, S, C, Z = multiply, near_plain, near_sum, reduce_own, reduce_z
    D, F, T = relay_z, forward, send_tokens
    order = (
        (gathered, 0), (M, 0), (B, 0), (left_step, 3), (S, 0),
        (M, 1), (B, 1), (left_step, 4), (S, 1), (C, 0),
        (F, 3), (T, 4), (M, 2), (B, 2), (S, 2), (D, 0), (C, 1),
        (F, 4), (right_send, 0), (M, 3), (B, 3), (S, 3), (D, 1), (C, 2), (Z, 0),
        (M, 4), (B, 4), (S, 4), (D, 2), (C, 3), (Z, 1), (right_cross, 0),
        (Z, 2), (D, 3), (C, 4), (Z, 3), (left_most, 0), (Z, 4),
    )
    for step, kc in order:
        step(kc)

    for kc in range(4, CHUNKS):
        arrived(g_full.at[other, rows_of(kc)], g_recv.at[kc])
    place = pl.ds(pl.multiple_of(z * 128, 128), 128)
    for way in range(2):
        some = slice(32 * way, 32 * way + 32)
        product = lg_f[way] + left_times(way, 384, HALF)
        lg_s[:, some] = product.astype(BF16).reshape(NZ, 32, 128)
        for step in FAR_FIRST:
            zt = ring(z, step, NZ)
            send(lg_s.at[zt, some], xm.at[some, place], t1_send, t1_recv.at[way],
                 device(x, y, zt, core))
        xm[some, place] = lg_s[z, some]
    arrived(rm.at[y_hi * 2 + other], r_recv.at[1])
    arrived(rm.at[far + other], r_recv.at[2])

    block = 2 * y + lax.div(x, 2)
    for xl in range(2):
        some = slice(32 * xl, 32 * xl + 32)
        arrived(lg_s.at[0:NZ - 1, some], t1_recv.at[xl])
        for yh in range(2):
            for cc in range(2):
                t = yh * 2 + cc
                result = jnp.dot(
                    xm[some], rm[:, :, t * 256:(t + 1) * 256].reshape(1024, 256),
                    preferred_element_type=F32,
                )
                first = xl * 8 + t * 2
                out_s[first:first + 2] = result.reshape(2, 16, 256)
                for yl in range(2):
                    is_me = jnp.logical_and(
                        jnp.logical_and(x == 2 * core + xl, y == 2 * yh + yl), core == cc
                    )
                    send_or_copy(is_me, out_s.at[first + yl], out_ref.at[mine, block],
                                 t2_send, t2_recv, device(2 * core + xl, 2 * yh + yl, z, cc))

    sent(tt.at[0:3], tk_send)
    sent(tt.at[3, 0], tk_send)
    sent(fw, tf_send)
    sent(dga.at[0], dg_send)
    sent(dga.at[0, 0], dg_send)
    sent(dga.at[0:2], dx_send)
    sent(a_s, a_send)
    sent(b_s, bb_send)
    sent(z_s.at[0:NZ - 1], zz_send)
    sent(g_full.at[0], g_send)
    sent(lb.at[0:NZ - 1], l3_send)
    sent(rm.at[0:3], r_send)
    sent(lg_s.at[0:NZ - 1], t1_send)
    sent(l1.at[0:3], l1_send)
    pl.when(jnp.logical_not(jnp.logical_and(y == y_t, core == l_core)))(
        lambda: sent(l1.at[3], l1_send)
    )
    arrived(out_ref, t2_recv)
    sent(out_s.at[0:15], t2_send)
    pl.when(core != l_core)(lambda: sent(out_s.at[15], t2_send))


def local(tokens, gate_pre, up_pre, d_hidden, left_roots, right_roots):
    dma = pltpu.SemaphoreType.DMA
    vm = pltpu.VMEM
    scratch = [
        vm((128, 8192), BF16), vm((512, 256), BF16), vm((512, 256), BF16),
        vm((512, 256), BF16), vm((16, 2, 2, 1024), BF16),
        vm((4, 2, 2, 512, 256), BF16),
        vm((NY, 2, 2, HALF, 128), BF16),
        vm((2, HALF, 1024), BF16),
        vm((2, 2, HALF, 128), BF16),
        vm((4, HALF, 1024), F32),
        vm((HALF, 1024), BF16),
        vm((2, HALF // 2, 1024), BF16),
        vm((2, HALF, 1024), BF16),
        vm((2, HALF, 1024), BF16),
        vm((NZ, HALF, 128), BF16),
        vm((NZ - 1, HALF, 128), BF16),
        vm((HALF, 128), BF16),
        vm((2, HALF, 128), BF16),
        vm((4, 16, 1024), BF16),
        vm((NZ, 4, 16, 1024), BF16),
        vm((2, 256, 128), F32),
        vm((NZ, 64, 128), BF16),
        vm((64, 1024), BF16),
        vm((4, 256, 1024), BF16),
        vm((16, 16, 256), F32),
        dma, dma((6,)), dma, dma,
        dma, dma((CHUNKS,)), dma,
        dma((CHUNKS, 2)),
        dma, dma((CHUNKS, 2)), dma, dma((CHUNKS,)),
        dma, dma((CHUNKS,)), dma((CHUNKS,)), dma, dma((CHUNKS,)),
        dma, dma, dma, dma((NZ - 1,)), dma, dma((3,)),
        dma, dma((2,)), dma, dma, dma((6,)),
    ]
    out = pl.pallas_call(
        kernel,
        out_shape=jax.ShapeDtypeStruct((2, 8, 16, 256), F32),
        in_specs=[pl.BlockSpec(memory_space=pltpu.HBM)] * 6,
        out_specs=pl.BlockSpec(memory_space=pltpu.VMEM),
        scratch_shapes=scratch,
        compiler_params=pltpu.CompilerParams(
            collective_id=0, has_side_effects=True, vmem_limit_bytes=60 * 1024 * 1024
        ),
        cost_estimate=pl.CostEstimate(
            flops=4_500_000_000, bytes_accessed=8_000_000, transcendentals=131072
        ),
    )(tokens, gate_pre, up_pre, d_hidden, left_roots, right_roots)
    return out.transpose(2, 1, 0, 3)


def solution(mesh):
    in_specs = (
        P(("dp", "tensor"), None),
        P("dp", "tensor"),
        P("dp", "tensor"),
        P("dp", "tensor"),
        P("dp", None, None, None),
        P(None, "tensor", None),
    )
    out_specs = P("dp", None, None, "tensor")
    return jax.shard_map(local, mesh=mesh, in_specs=in_specs, out_specs=out_specs, check_vma=False)
```

```python
import jax
import jax.numpy as jnp
from jax import lax
from jax.experimental import pallas as pl
from jax.experimental.pallas import tpu as pltpu
from jax.sharding import PartitionSpec as P

MESH = pl.DeviceIdType.MESH
F32 = jnp.float32
BF16 = jnp.bfloat16

NX, NY, NZ = 4, 4, 8
SIZES = (96, 128, 128, 96, 64)
STARTS = tuple(sum(SIZES[:i]) for i in range(len(SIZES)))
CHUNKS = len(SIZES)
HALF = 512
FAR_FIRST = (4, 3, 5, 2, 6, 1, 7)


def device(x, y, z, core):
    return ((x * NZ + z) * 2 + lax.rem(y, 2), lax.div(y, 2) * 2 + core)


def ring(value, step, size):
    return lax.rem(value + (step + size), size)


def lane_of(y, core):
    return pl.multiple_of(
        lax.rem(y, 2) * 512 + (lax.div(y, 2) * 2 + core) * 128, 128
    )


def kernel(
    tok_hbm, gate_hbm, up_hbm, dh_hbm, left_hbm, right_hbm, out_ref,
    tok_ref, gate_ref, up_ref, dh_ref, left_ref, dga, tt, tk, fw, part, a_s, a_r, b_s, b_r, z_s, z_r, g_full,
    l1, lb, lg_f, lg_s, xm, rm, out_s,
    dg_send, dg_recv, dx_send, dx_recv, tk_send, tk_recv, tf_send,
    fw_recv, a_send, a_recv, bb_send, bb_recv, zz_send, zz_recv,
    g_send, g_recv, l1_send, l1_recv, l3_send, l3_recv, r_send, r_recv,
    t1_send, t1_recv, t2_send, t2_recv, in_sem,
):
    dp = lax.axis_index("dp")
    tensor = lax.axis_index("tensor")
    y_lo = lax.rem(dp, 2)
    z = lax.rem(lax.div(dp, 2), NZ)
    x = lax.div(dp, 2 * NZ)
    y_hi = lax.div(tensor, 2)
    core = lax.rem(tensor, 2)
    y = y_hi * 2 + y_lo
    other = 1 - core
    xp, xm1, xo = ring(x, 1, NX), ring(x, -1, NX), ring(x, 2, NX)
    yp, ym, yo = ring(y, 1, NY), ring(y, -1, NY), ring(y, 2, NY)

    def send(src, dst, ssem, rsem, dev):
        pltpu.make_async_remote_copy(
            src_ref=src, dst_ref=dst, send_sem=ssem, recv_sem=rsem,
            device_id=dev, device_id_type=MESH,
        ).start()

    def send_or_copy(is_me, src, dst, ssem, rsem, dev):
        @pl.when(is_me)
        def _():
            pltpu.make_async_copy(src, dst, rsem).start()

        @pl.when(jnp.logical_not(is_me))
        def _():
            send(src, dst, ssem, rsem, dev)

    def arrived(dst, rsem):
        pltpu.make_async_remote_copy(
            src_ref=dst, dst_ref=dst, send_sem=rsem, recv_sem=rsem,
            device_id=device(x, y, z, other), device_id_type=MESH,
        ).wait_recv()

    def sent(src, ssem):
        pltpu.make_async_remote_copy(
            src_ref=src, dst_ref=src, send_sem=ssem, recv_sem=ssem,
            device_id=device(x, y, z, other), device_id_type=MESH,
        ).wait_send()

    y_t = y_hi * 2 + core
    mine = lax.rem(x, 2)
    loads = [
        pltpu.make_async_copy(src, dst, in_sem.at[i])
        for i, (src, dst) in enumerate((
            (gate_hbm, gate_ref), (up_hbm, up_ref), (dh_hbm, dh_ref),
            (left_hbm.at[:, pl.ds(2 * y_t, 2)], left_ref), (tok_hbm, tok_ref),
            (right_hbm.at[mine], rm.at[tensor]),
        ))
    ]
    for load in loads:
        load.start()

    barrier = pltpu.get_barrier_semaphore()
    partners = []
    for step_x in range(NX):
        for step_y in range(NY):
            for cc in range(2):
                if step_x or step_y or cc:
                    partners.append(device(
                        ring(x, step_x, NX), ring(y, step_y, NY), z, lax.rem(core + cc, 2)
                    ))
    for step in range(1, NZ):
        partners.append(device(x, y, ring(z, step, NZ), core))
    for partner in partners:
        pl.semaphore_signal(barrier, inc=1, device_id=partner, device_id_type=MESH)

    def elementwise(i, _):
        rows = pl.ds(pl.multiple_of(i * 64, 64), 64)
        g = gate_ref[rows, :].astype(F32)
        u = up_ref[rows, :].astype(F32)
        h = dh_ref[rows, :].astype(F32)
        s = 1.0 / (1.0 + jnp.exp(-g))
        dga[tensor, 0, y_lo, rows, :] = (h * u * s * (1.0 + g * (1.0 - s))).astype(BF16)
        dga[tensor, 1, y_lo, rows, :] = (h * g * s).astype(BF16)
        return 0

    for load in loads[:3]:
        load.wait()
    lax.fori_loop(0, 8, elementwise, 0)
    pl.semaphore_wait(barrier, len(partners))

    def dg(y_from, m):
        return dga.at[lax.div(y_from, 2) * 2 + core, m, lax.rem(y_from, 2)]

    def along(y_from, m, index, y_to):
        send(dg(y_from, m), dg(y_from, m), dg_send, dg_recv.at[index], device(x, y_to, z, core))

    def cross(y_from, m):
        send(dg(y_from, m), dg(y_from, m), dx_send, dx_recv, device(x, y, z, other))

    along(y, 0, 0, yp)
    along(y, 1, 1, ym)
    along(y, 1, 2, yp)
    along(y, 0, 3, ym)
    cross(y, 0)
    cross(y, 1)

    loads[3].wait()
    l_core = lax.div(x, 2)
    l_slot = lax.rem(x, 2) * 2 + y_lo
    for x_t in range(NX):
        is_me = jnp.logical_and(jnp.logical_and(x == x_t, y == y_t), core == l_core)
        l1[x_t] = left_ref[:, x_t // 2, x_t % 2]
        send_or_copy(is_me, l1.at[x_t], lb.at[z, l_slot], l1_send, l1_recv,
                     device(x_t, y_t, z, l_core))

    loads[4].wait()

    def transpose(y_to, _):
        for bl in range(2):
            for cc in range(2):
                for part_of in range(4):
                    column = pl.multiple_of(
                        y_to * 2048 + (bl * 1024 + cc * 512 + part_of * 128), 128
                    )
                    tt[y_to, bl, cc, part_of * 128:(part_of + 1) * 128] = (
                        tok_ref[:, pl.ds(column, 128)].T
                    )
        return 0

    lax.fori_loop(0, NY, transpose, 0)

    def rows_of(kc):
        return pl.ds(STARTS[kc], SIZES[kc])

    def send_tokens(kc):
        rows = rows_of(kc)
        here = tk.at[:, rows, pl.ds(lane_of(y, core), 128)]
        send(tt.at[yo, 0, :, rows], fw.at[0, :, rows], tk_send, fw_recv.at[kc, 0],
             device(x, yp, z, core))
        send(tt.at[yo, 1, :, rows], fw.at[1, :, rows], tk_send, fw_recv.at[kc, 1],
             device(x, ym, z, core))
        for cc in range(2):
            send(tt.at[yp, :, cc, rows], here, tk_send, tk_recv.at[kc], device(x, yp, z, cc))
            send(tt.at[ym, :, cc, rows], here, tk_send, tk_recv.at[kc], device(x, ym, z, cc))
        send(tt.at[y, :, other, rows], here, tk_send, tk_recv.at[kc], device(x, y, z, other))
        pltpu.make_async_copy(tt.at[y, :, core, rows], here, tk_recv.at[kc]).start()

    def forward(kc):
        rows = rows_of(kc)
        for way, y_from, y_to in ((0, ym, yp), (1, yp, ym)):
            arrived(fw.at[way, :, rows], fw_recv.at[kc, way])
            there = tk.at[way, rows, pl.ds(lane_of(y_from, core), 128)]
            for cc in range(2):
                send(fw.at[way, cc, rows], there, tf_send, tk_recv.at[kc],
                     device(x, y_to, z, cc))

    arrived(dg(ym, 0), dg_recv.at[0])
    along(ym, 0, 4, yp)
    arrived(dg(yp, 1), dg_recv.at[1])
    along(yp, 1, 5, ym)
    cross(ym, 0)
    cross(yp, 1)

    zp, zm = ring(z, 1, NZ), ring(z, -1, NZ)

    def left_up(step):
        slot = ring(z, -step, NZ)
        if step > 0:
            arrived(lb.at[slot], l3_recv.at[step - 1])
        if step < 4:
            send(lb.at[slot], lb.at[slot], l3_send, l3_recv.at[step],
                 device(x, y, zp, core))

    def left_down(step):
        slot = ring(z, step, NZ)
        if step > 0:
            arrived(lb.at[slot], l3_recv.at[3 + step])
        if step < 3:
            send(lb.at[slot], lb.at[slot], l3_send, l3_recv.at[4 + step],
                 device(x, y, zm, core))

    def left_step(step):
        left_up(step)
        if step < 4:
            left_down(step)

    send_tokens(0)
    arrived(lb.at[z], l1_recv)
    left_step(0)
    arrived(dg(ym, 1), dg_recv.at[2])
    cross(ym, 1)
    arrived(dg(yp, 0), dg_recv.at[3])
    cross(yp, 0)
    left_step(1)

    arrived(dg(yo, 0), dg_recv.at[4])
    cross(yo, 0)
    arrived(dg(yo, 1), dg_recv.at[5])
    cross(yo, 1)
    forward(0)
    send_tokens(1)
    left_step(2)

    def multiply(kc):
        rows, size = rows_of(kc), SIZES[kc]
        arrived(tk.at[:, rows], tk_recv.at[kc])

        def matrix(turn, _):
            m = lax.rem(mine + turn, 2)
            for t in range(4):
                total = jnp.dot(
                    tk[:, rows].reshape(2 * size, 1024), dga[t, m].reshape(1024, 256),
                    preferred_element_type=F32,
                )
                for bl in range(2):
                    part[bl * 2 + m, rows, t * 256:(t + 1) * 256] = (
                        total[bl * size:(bl + 1) * size]
                    )

            @pl.when(turn == 0)
            def _():
                reduce_far(kc)
                if kc < 2:
                    forward(kc + 1)
                    send_tokens(kc + 2)

            return 0

        lax.fori_loop(0, 2, matrix, 0)

    def halves(kc):
        start, half = STARTS[kc], SIZES[kc] // 2
        return pl.ds(start, half), pl.ds(start + half, half), pl.ds(start // 2, half)

    def reduce_far(kc):
        rows = rows_of(kc)
        first, second, packed = halves(kc)
        a_s[rows] = part[xo, rows].astype(BF16)
        send(a_s.at[first], a_r.at[0, packed], a_send, a_recv.at[kc, 0],
             device(xp, y, z, core))
        send(a_s.at[second], a_r.at[1, packed], a_send, a_recv.at[kc, 1],
             device(xm1, y, z, core))

    def near_plain(kc):
        first, second, _ = halves(kc)
        for way, x_to, plain in ((0, xp, second), (1, xm1, first)):
            b_s[way, plain] = part[x_to, plain].astype(BF16)
            send(b_s.at[way, plain], b_r.at[way, plain], bb_send, bb_recv.at[kc],
                 device(x_to, y, z, core))

    def near_sum(kc):
        first, second, packed = halves(kc)
        for way, x_to, summed in ((0, xp, first), (1, xm1, second)):
            arrived(a_r.at[way, packed], a_recv.at[kc, way])
            b_s[way, summed] = (
                part[x_to, summed] + a_r[way, packed].astype(F32)
            ).astype(BF16)
            send(b_s.at[way, summed], b_r.at[way, summed], bb_send, bb_recv.at[kc],
                 device(x_to, y, z, core))

    def reduce_own(kc):
        rows = rows_of(kc)
        arrived(b_r.at[:, rows], bb_recv.at[kc])
        for zt in range(NZ):
            cols = slice(zt * 128, (zt + 1) * 128)
            z_s[zt, rows] = (
                part[x, rows, cols]
                + b_r[0, rows, cols].astype(F32)
                + b_r[1, rows, cols].astype(F32)
            ).astype(BF16)
        for step in FAR_FIRST:
            zt = ring(z, step, NZ)
            send(z_s.at[zt, rows], z_r.at[step - 1, rows], zz_send,
                 zz_recv.at[kc], device(x, y, zt, core))

    def reduce_z(kc):
        rows = rows_of(kc)
        arrived(z_r.at[:, rows], zz_recv.at[kc])
        total = z_s[z, rows].astype(F32)
        for i in range(NZ - 1):
            total = total + z_r[i, rows].astype(F32)
        g_full[core, rows] = total.astype(BF16)
        send(g_full.at[core, rows], g_full.at[core, rows], g_send, g_recv.at[kc],
             device(x, y, z, other))

    far = (1 - y_hi) * 2

    def right_send(_):
        loads[5].wait()
        send(rm.at[tensor], rm.at[tensor], r_send, r_recv.at[0],
             device(x, NY - 1 - y, z, core))
        send(rm.at[tensor], rm.at[tensor], r_send, r_recv.at[1],
             device(x, y, z, other))

    def right_cross(_):
        arrived(rm.at[far + core], r_recv.at[0])
        send(rm.at[far + core], rm.at[far + core], r_send, r_recv.at[2],
             device(x, y, z, other))

    def left_times(way, low, high):
        return sum(
            jnp.dot(
                lb[:, 2 * way:2 * way + 2, :, cc * HALF + low:cc * HALF + high].reshape(
                    256, high - low
                ),
                g_full[cc, low:high], preferred_element_type=F32,
            )
            for cc in range(2)
        )

    def left_most(_):
        for kc in range(4):
            arrived(g_full.at[other, rows_of(kc)], g_recv.at[kc])
        for way in range(2):
            lg_f[way] = left_times(way, 0, 384)

    def gathered(_):
        arrived(dga.at[0:2], dx_recv)

    M, B, S, C, Z = multiply, near_plain, near_sum, reduce_own, reduce_z
    F, T = forward, send_tokens
    order = (
        (gathered, 0), (M, 0), (B, 0), (left_step, 3), (S, 0),
        (M, 1), (B, 1), (left_step, 4), (C, 0), (S, 1),
        (F, 3), (T, 4), (M, 2), (B, 2), (C, 1), (S, 2), (Z, 0),
        (F, 4), (right_send, 0), (M, 3), (B, 3), (C, 2), (S, 3), (Z, 1),
        (M, 4), (B, 4), (C, 3), (S, 4), (Z, 2), (right_cross, 0),
        (C, 4), (Z, 3), (left_most, 0), (Z, 4),
    )
    for step, kc in order:
        step(kc)

    for kc in range(4, CHUNKS):
        arrived(g_full.at[other, rows_of(kc)], g_recv.at[kc])
    place = pl.ds(pl.multiple_of(z * 128, 128), 128)
    for way in range(2):
        some = slice(32 * way, 32 * way + 32)
        product = lg_f[way] + left_times(way, 384, HALF)
        lg_s[:, some] = product.astype(BF16).reshape(NZ, 32, 128)
        for step in FAR_FIRST:
            zt = ring(z, step, NZ)
            send(lg_s.at[zt, some], xm.at[some, place], t1_send, t1_recv.at[way],
                 device(x, y, zt, core))
        xm[some, place] = lg_s[z, some]
    arrived(rm.at[y_hi * 2 + other], r_recv.at[1])
    arrived(rm.at[far + other], r_recv.at[2])

    block = 2 * y + lax.div(x, 2)
    for xl in range(2):
        some = slice(32 * xl, 32 * xl + 32)
        arrived(lg_s.at[0:NZ - 1, some], t1_recv.at[xl])
        for yh in range(2):
            for cc in range(2):
                t = yh * 2 + cc
                result = jnp.dot(
                    xm[some], rm[:, :, t * 256:(t + 1) * 256].reshape(1024, 256),
                    preferred_element_type=F32,
                )
                first = xl * 8 + t * 2
                out_s[first:first + 2] = result.reshape(2, 16, 256)
                for yl in range(2):
                    is_me = jnp.logical_and(
                        jnp.logical_and(x == 2 * core + xl, y == 2 * yh + yl), core == cc
                    )
                    send_or_copy(is_me, out_s.at[first + yl], out_ref.at[mine, block],
                                 t2_send, t2_recv, device(2 * core + xl, 2 * yh + yl, z, cc))

    sent(tt.at[0:3], tk_send)
    sent(tt.at[3, 0], tk_send)
    sent(fw, tf_send)
    sent(dga.at[0], dg_send)
    sent(dga.at[0, 0], dg_send)
    sent(dga.at[0:2], dx_send)
    sent(a_s, a_send)
    sent(b_s, bb_send)
    sent(z_s.at[0:NZ - 1], zz_send)
    sent(g_full.at[0], g_send)
    sent(lb.at[0:NZ - 1], l3_send)
    sent(rm.at[0:3], r_send)
    sent(lg_s.at[0:NZ - 1], t1_send)
    sent(l1.at[0:3], l1_send)
    pl.when(jnp.logical_not(jnp.logical_and(y == y_t, core == l_core)))(
        lambda: sent(l1.at[3], l1_send)
    )
    arrived(out_ref, t2_recv)
    sent(out_s.at[0:15], t2_send)
    pl.when(core != l_core)(lambda: sent(out_s.at[15], t2_send))


def local(tokens, gate_pre, up_pre, d_hidden, left_roots, right_roots):
    dma = pltpu.SemaphoreType.DMA
    vm = pltpu.VMEM
    scratch = [
        vm((128, 8192), BF16), vm((512, 256), BF16), vm((512, 256), BF16),
        vm((512, 256), BF16), vm((16, 2, 2, 1024), BF16),
        vm((4, 2, 2, 512, 256), BF16),
        vm((NY, 2, 2, HALF, 128), BF16),
        vm((2, HALF, 1024), BF16),
        vm((2, 2, HALF, 128), BF16),
        vm((4, HALF, 1024), F32),
        vm((HALF, 1024), BF16),
        vm((2, HALF // 2, 1024), BF16),
        vm((2, HALF, 1024), BF16),
        vm((2, HALF, 1024), BF16),
        vm((NZ, HALF, 128), BF16),
        vm((NZ - 1, HALF, 128), BF16),
        vm((2, HALF, 128), BF16),
        vm((4, 16, 1024), BF16),
        vm((NZ, 4, 16, 1024), BF16),
        vm((2, 256, 128), F32),
        vm((NZ, 64, 128), BF16),
        vm((64, 1024), BF16),
        vm((4, 256, 1024), BF16),
        vm((16, 16, 256), F32),
        dma, dma((6,)), dma, dma,
        dma, dma((CHUNKS,)), dma,
        dma((CHUNKS, 2)),
        dma, dma((CHUNKS, 2)), dma, dma((CHUNKS,)),
        dma, dma((CHUNKS,)), dma, dma((CHUNKS,)),
        dma, dma, dma, dma((NZ - 1,)), dma, dma((3,)),
        dma, dma((2,)), dma, dma, dma((6,)),
    ]
    out = pl.pallas_call(
        kernel,
        out_shape=jax.ShapeDtypeStruct((2, 8, 16, 256), F32),
        in_specs=[pl.BlockSpec(memory_space=pltpu.HBM)] * 6,
        out_specs=pl.BlockSpec(memory_space=pltpu.VMEM),
        scratch_shapes=scratch,
        compiler_params=pltpu.CompilerParams(
            collective_id=0, has_side_effects=True, vmem_limit_bytes=60 * 1024 * 1024
        ),
        cost_estimate=pl.CostEstimate(
            flops=4_500_000_000, bytes_accessed=8_000_000, transcendentals=131072
        ),
    )(tokens, gate_pre, up_pre, d_hidden, left_roots, right_roots)
    return out.transpose(2, 1, 0, 3)


def solution(mesh):
    in_specs = (
        P(("dp", "tensor"), None),
        P("dp", "tensor"),
        P("dp", "tensor"),
        P("dp", "tensor"),
        P("dp", None, None, None),
        P(None, "tensor", None),
    )
    out_specs = P("dp", None, None, "tensor")
    return jax.shard_map(local, mesh=mesh, in_specs=in_specs, out_specs=out_specs, check_vma=False)
```
